128 devices in a mesh: role: 2 (over core), shard: 64 (over x, y, z).
Axes of the slice: x: 4, y: 4, z: 4, core: 2. Of those that a mesh axis runs over, the one named last changes fastest.
Arguments:
- query: bfloat16 [512, 8192], P('shard', 'role'), may hold values from -5 to 5, as said below
- fresh_token_keys: bfloat16 [512, 512], P('shard', 'role'), may hold values from -4 to 4
- fresh_token_values: bfloat16 [512, 512], P('shard', 'role'), may hold values from -4 to 4
- stored_keys: bfloat16 [512, 1024, 512], P('shard', None, 'role'), may hold values from -5 to 5, as said below
- stored_values: bfloat16 [512, 1024, 512], P('shard', None, 'role'), may hold values from -4 to 4
- slot_cache_length: int32 [512], P('shard'), may hold values from 2 to 1024, as said below
- residual: bfloat16 [512, 8192], P('shard', 'role'), may hold values from -6 to 6
- prenorm_scale: bfloat16 [8192], replicated, may hold values from 0.5 to 1.5
- request_cache_slot: int32 [512], replicated, may hold values from 0 to 511, each once
- request_adapter: int32 [512], replicated, may hold values from 0 to 255
- gate_projection_levels: bfloat16 [8192, 32768], P(None, ('role', 'shard')), may hold values from -8 to 7, as said below
- gate_group_scales: float32 [64, 32768], P(None, ('role', 'shard')), may hold values from 0.0012153398 to 0.0049718446
- up_projection_levels: bfloat16 [8192, 32768], P(None, ('role', 'shard')), may hold values from -8 to 7, as said below
- up_group_scales: float32 [64, 32768], P(None, ('role', 'shard')), may hold values from 0.0012153398 to 0.0049718446
- down_projection_levels: bfloat16 [32768, 8192], P(('role', 'shard')), may hold values from -8 to 7, as said below
- down_group_scales: float32 [256, 8192], P(('role', 'shard')), may hold values from 0.0006076699 to 0.002375437
- adapter_input_maps: bfloat16 [256, 16, 8192], P(('role', 'shard')), may hold values from -0.0625 to 0.0625
- adapter_gate_maps: bfloat16 [256, 16, 32768], P(None, None, ('role', 'shard')), may hold values from -1.5 to 1.5
Outputs:
- layer_out: bfloat16 [512, 8192], P(('role', 'shard'))
The draws below stay inside these ranges and needn't reach their ends.
Inputs may be any that keep to these rules, and one draw needn't show every extreme that they name: `query`: entries are bounded in size. `stored_keys`: entries are bounded in size. `slot_cache_length`: some slot holds exactly 1024 cached tokens. `gate_projection_levels`: whole numbers. `up_projection_levels`: whole numbers. `down_projection_levels`: whole numbers.
All inputs are finite; a program needn't handle non-finite values.
Results may differ from the reference program's by a relative error of at most 0.01.
Values may be sent and summed in bfloat16 or wider, within the bound.
No kernel may reach another device: no remote copies, remote signals or barrier semaphores. Data moves between devices by JAX's collectives and lax.ppermute only.
A program may use at most 192 MiB of HBM per device.

```python
import math
import jax
import jax.numpy as jnp
import numpy as np
from jax import lax

HQ = 64
KVH = 4
HD = 128
MODEL_WIDTH = 8192
HIDDEN_UNITS = 32768
GROUP = 128
ADAPTER_COUNT = 256
ADAPTER_RANK = 16
LEN = 1024
ROWS = 512
KV = 512


def draw_query(key, part):
    key = jax.random.fold_in(key, 1)
    base = jax.random.truncated_normal(key, -4.0, 4.0, (ROWS, HQ, HD), jnp.float32)
    return base.reshape(ROWS, HQ * HD).astype(jnp.bfloat16)


def draw_stored_keys(key, part):
    key = jax.random.fold_in(key, 2)
    base = jax.random.truncated_normal(key, -4.0, 4.0, (ROWS, LEN, KVH, HD), jnp.float32)
    return base.reshape(ROWS, LEN, KVH * HD).astype(jnp.bfloat16)


def draw_slot_cache_length(key, part):
    key = jax.random.fold_in(key, 3)
    key_len, key_pick = jax.random.split(key)
    lengths = jax.random.randint(key_len, (ROWS,), 2, LEN + 1)
    pick = jax.random.randint(key_pick, (), 0, ROWS)
    return lengths.at[pick].set(LEN).astype(jnp.int32)


def draw_gate_projection_levels(key, part):
    key = jax.random.fold_in(key, 4)
    return jax.random.randint(key, (MODEL_WIDTH, HIDDEN_UNITS), -8, 8).astype(jnp.float32).astype(jnp.bfloat16)


def draw_up_projection_levels(key, part):
    key = jax.random.fold_in(key, 5)
    return jax.random.randint(key, (MODEL_WIDTH, HIDDEN_UNITS), -8, 8).astype(jnp.float32).astype(jnp.bfloat16)


def draw_down_projection_levels(key, part):
    key = jax.random.fold_in(key, 6)
    return jax.random.randint(key, (HIDDEN_UNITS, MODEL_WIDTH), -8, 8).astype(jnp.float32).astype(jnp.bfloat16)


def set_ends(result, stream_key, least, largest):
    spot = [jax.random.randint(jax.random.fold_in(stream_key, axis), (), 0, length) for axis, length in enumerate(result.shape)]
    widest = result.shape.index(max(result.shape))
    beside = spot[:widest] + [(spot[widest] + 1) % result.shape[widest]] + spot[widest + 1:]
    return result.at[tuple(spot)].set(least).at[tuple(beside)].set(largest)


def level_of(rng, extent, shards, least, top_value):
    def one(dim, parts):
        draws = jax.random.uniform(jax.random.fold_in(jax.random.fold_in(rng, 6), dim), (parts,), jnp.float32, least / len(shards), top_value / len(shards))
        return jnp.repeat(jnp.exp(draws), extent[dim] // parts).reshape((-1,) + (1,) * (len(extent) - dim - 1))

    factor_of = one(*shards[0])
    for cut in shards[1:]:
        factor_of = factor_of * one(*cut)
    return factor_of


def cumulative_ranks(number_of, skew):
    loads = [(1 << 20) // math.isqrt(grade ** skew) + 1 for grade in range(1, number_of + 1)]
    deviation = 1 + sum(loads) // (1 << 30)
    return np.cumsum(np.array([max(1, weight // deviation) for weight in loads]))


def skewed_ids(own_key, extent, number_of, lean):
    table = cumulative_ranks(number_of, lean)
    ticket = jax.random.randint(jax.random.fold_in(own_key, 1), extent, 0, int(table[number_of - 1]))
    rank = jnp.searchsorted(jnp.asarray(table, jnp.int32), ticket, side="right")
    return jax.random.permutation(jax.random.fold_in(own_key, 2), number_of)[rank].astype(jnp.int32)


def scatter_about(stream_key, dims, scale, bound, cuts=(), kind=jnp.bfloat16):
    drawn = jax.random.normal(stream_key, dims, jnp.float32) * scale
    if len(cuts) > 0:
        drawn = level_of(stream_key, dims, cuts, -0.22, 0.18) * drawn
    return jnp.clip(drawn, min=-bound, max=bound).astype(kind)


def setup_inputs(seed: int = 0) -> dict:
    splits = jax.random.split(jax.random.key(seed), 19)
    query = draw_query(jax.random.fold_in(splits[18], 71), 0)
    fresh_token_keys = scatter_about(splits[1], (ROWS, KV), 1.0, 4.0, ((0, 64), (1, 2)))
    fresh_token_values = scatter_about(splits[2], (ROWS, KV), 1.0, 4.0, ((0, 64), (1, 2)))
    stored_keys = draw_stored_keys(jax.random.fold_in(splits[18], 71), 0)
    stored_values = scatter_about(splits[4], (ROWS, LEN, KV), 1.0, 4.0, ((0, 64), (2, 2)))
    slot_cache_length = draw_slot_cache_length(jax.random.fold_in(splits[18], 71), 0)
    residual = scatter_about(splits[6], (ROWS, MODEL_WIDTH), 1.0, 6.0, ((0, 64), (1, 2)))
    prenorm_scale = jnp.clip(1.0 + 0.1 * jax.random.normal(splits[7], (MODEL_WIDTH,), jnp.float32), 0.5, 1.5).astype(jnp.bfloat16)
    request_cache_slot = jax.random.permutation(splits[8], ROWS).astype(jnp.int32)
    request_adapter = set_ends(skewed_ids(splits[9], (ROWS,), ADAPTER_COUNT, 2), jax.random.fold_in(splits[9], 3), 0, ADAPTER_COUNT - 1).astype(jnp.int32)
    gate_projection_levels = draw_gate_projection_levels(jax.random.fold_in(splits[18], 71), 0)
    gate_group_scales = jnp.clip(jnp.exp(math.log(0.0049718446) - 1.4087672 * jax.random.uniform(splits[11], (MODEL_WIDTH // GROUP, HIDDEN_UNITS), jnp.float32) ** level_of(splits[11], (MODEL_WIDTH // GROUP, HIDDEN_UNITS), ((1, 128),), -0.2, 0.2)), 0.0012153398, 0.0049718446)
    up_projection_levels = draw_up_projection_levels(jax.random.fold_in(splits[18], 71), 0)
    up_group_scales = jnp.clip(jnp.exp(math.log(0.0049718446) - 1.4087672 * jax.random.uniform(splits[13], (MODEL_WIDTH // GROUP, HIDDEN_UNITS), jnp.float32) ** level_of(splits[13], (MODEL_WIDTH // GROUP, HIDDEN_UNITS), ((1, 128),), -0.2, 0.2)), 0.0012153398, 0.0049718446)
    down_projection_levels = draw_down_projection_levels(jax.random.fold_in(splits[18], 71), 0)
    down_group_scales = jnp.clip(jnp.exp(math.log(0.002375437) - 1.3633049 * jax.random.uniform(splits[15], (HIDDEN_UNITS // GROUP, MODEL_WIDTH), jnp.float32) ** level_of(splits[15], (HIDDEN_UNITS // GROUP, MODEL_WIDTH), ((0, 128),), -0.2, 0.2)), 0.0006076699, 0.002375437)
    adapter_input_maps = scatter_about(splits[16], (ADAPTER_COUNT, ADAPTER_RANK, MODEL_WIDTH), MODEL_WIDTH ** -0.5, 0.0625, ((0, 128),))
    adapter_gate_maps = scatter_about(splits[17], (ADAPTER_COUNT, ADAPTER_RANK, HIDDEN_UNITS), ADAPTER_RANK ** -0.5, 1.5, ((2, 128),))
    return dict(query=query, fresh_token_keys=fresh_token_keys, fresh_token_values=fresh_token_values, stored_keys=stored_keys, stored_values=stored_values, slot_cache_length=slot_cache_length, residual=residual, prenorm_scale=prenorm_scale, request_cache_slot=request_cache_slot, request_adapter=request_adapter, gate_projection_levels=gate_projection_levels, gate_group_scales=gate_group_scales, up_projection_levels=up_projection_levels, up_group_scales=up_group_scales, down_projection_levels=down_projection_levels, down_group_scales=down_group_scales, adapter_input_maps=adapter_input_maps, adapter_gate_maps=adapter_gate_maps)


def attend(query, fresh_token_keys, fresh_token_values, stored_keys, stored_values, slot_cache_length, kv_heads, head_dim):
    rows = query.shape[0]
    length = stored_keys.shape[1]
    groups = query.shape[1] // (kv_heads * head_dim)
    queries = query.reshape(rows, kv_heads, groups, head_dim).astype(jnp.float32)
    keys = stored_keys.reshape(rows, length, kv_heads, head_dim).astype(jnp.float32)
    values = stored_values.reshape(rows, length, kv_heads, head_dim).astype(jnp.float32)
    own_keys = fresh_token_keys.reshape(rows, kv_heads, head_dim).astype(jnp.float32)
    own_values = fresh_token_values.reshape(rows, kv_heads, head_dim).astype(jnp.float32)
    factor = head_dim ** (-0.5)
    scores = jnp.einsum('skgd,slkd->skgl', queries, keys) * factor
    valid = jnp.arange(length)[None, :] < slot_cache_length[:, None]
    scores = jnp.where(valid[:, None, None, :], scores, -1e+30)
    own = jnp.einsum('skgd,skd->skg', queries, own_keys) * factor
    top = jnp.maximum(lax.optimization_barrier(jnp.max(scores, axis=-1)), own)
    weights = jnp.exp(scores - top[..., None])
    own_weight = jnp.exp(own - top)
    total = lax.optimization_barrier(jnp.sum(weights, axis=-1)) + own_weight
    mixed = jnp.einsum('skgl,slkd->skgd', weights.astype(jnp.bfloat16).astype(jnp.float32), values)
    mixed = mixed + own_weight.astype(jnp.bfloat16).astype(jnp.float32)[..., None] * own_values[:, :, None, :]
    return (mixed / total[..., None]).reshape(rows, -1)

def dequant(levels, scales):
    count, cols = levels.shape
    blocks = scales.shape[0]
    wide = levels.reshape(blocks, count // blocks, cols).astype(jnp.float32) * scales[:, None, :]
    return wide.reshape(count, cols).astype(jnp.bfloat16)

def norm_rows(stream, prenorm_scale):
    wide = stream.astype(jnp.float32)
    meansq = lax.optimization_barrier(jnp.mean(wide * wide, axis=-1, keepdims=True))
    return (wide * lax.rsqrt(meansq + 1e-05) * prenorm_scale.astype(jnp.float32)).astype(jnp.bfloat16)

def reference(query, fresh_token_keys, fresh_token_values, stored_keys, stored_values, slot_cache_length, residual, prenorm_scale, request_cache_slot, request_adapter, gate_projection_levels, gate_group_scales, up_projection_levels, up_group_scales, down_projection_levels, down_group_scales, adapter_input_maps, adapter_gate_maps):
    attended = attend(query, fresh_token_keys, fresh_token_values, stored_keys, stored_values, slot_cache_length, KVH, HD)
    stream = (residual.astype(jnp.float32) + attended).astype(jnp.bfloat16)
    normed = norm_rows(stream, prenorm_scale)
    sorted_entries = jnp.take(normed, request_cache_slot, axis=0)
    w_gate = dequant(gate_projection_levels, gate_group_scales)
    w_up = dequant(up_projection_levels, up_group_scales)
    w_down = dequant(down_projection_levels, down_group_scales)
    block = 32
    count = ROWS // block

    def one_block(index):
        start = index * block
        x_blk = lax.dynamic_slice_in_dim(sorted_entries, start, block, 0)
        identifiers = lax.dynamic_slice_in_dim(request_adapter, start, block, 0)
        selected_down_map = jnp.take(adapter_input_maps, identifiers, axis=0).astype(jnp.float32)
        low = jnp.einsum('nd,nrd->nr', x_blk.astype(jnp.float32), selected_down_map).astype(jnp.bfloat16)
        selected_up_map = jnp.take(adapter_gate_maps, identifiers, axis=0).astype(jnp.float32)
        delta = jnp.einsum('nr,nrf->nf', low.astype(jnp.float32), selected_up_map)
        gate = jnp.dot(x_blk, w_gate, preferred_element_type=jnp.float32) + 2.0 * delta
        up = jnp.dot(x_blk, w_up, preferred_element_type=jnp.float32)
        hidden = (jax.nn.silu(gate) * up).astype(jnp.bfloat16)
        down = jnp.dot(hidden, w_down, preferred_element_type=jnp.float32)
        own_stream = jnp.take(stream, lax.dynamic_slice_in_dim(request_cache_slot, start, block, 0), axis=0)
        return (own_stream.astype(jnp.float32) + down).astype(jnp.bfloat16)
    pieces = lax.map(one_block, jnp.arange(count, dtype=jnp.int32))
    return pieces.reshape(ROWS, MODEL_WIDTH)
```

```python
import functools

import jax
import jax.numpy as jnp
from jax import lax
from jax.experimental import pallas as pl
from jax.experimental.pallas import tpu as pltpu
from jax.sharding import PartitionSpec as P

HD = 128
BF = jnp.bfloat16
F32 = jnp.float32
AXES = ((2, 1, 0), (2, 0, 1))


def attend(
    query,
    fresh_token_keys,
    fresh_token_values,
    stored_keys,
    stored_values,
    slot_cache_length,
    kv_heads,
    head_dim,
):
    rows = query.shape[0]
    length = stored_keys.shape[1]
    groups = query.shape[1] // (kv_heads * head_dim)
    queries = query.reshape(rows, kv_heads, groups, head_dim)
    keys = stored_keys.reshape(rows, length, kv_heads, head_dim)
    values = stored_values.reshape(rows, length, kv_heads, head_dim)
    own_keys = fresh_token_keys.reshape(rows, kv_heads, head_dim)
    own_values = fresh_token_values.reshape(rows, kv_heads, head_dim)
    factor = head_dim ** (-0.5)
    scores = jnp.einsum("skgd,slkd->skgl", queries, keys, preferred_element_type=F32) * factor
    valid = jnp.arange(length)[None, :] < slot_cache_length[:, None]
    scores = jnp.where(valid[:, None, None, :], scores, -1e30)
    own = jnp.einsum("skgd,skd->skg", queries, own_keys, preferred_element_type=F32) * factor
    top = jnp.maximum(jnp.max(scores, axis=-1), own)
    weights = jnp.exp(scores - top[..., None])
    own_weight = jnp.exp(own - top)
    total = jnp.sum(weights, axis=-1) + own_weight
    mixed = jnp.einsum("skgl,slkd->skgd", weights.astype(BF), values, preferred_element_type=F32)
    mixed = (
        mixed
        + own_weight.astype(BF).astype(F32)[..., None] * own_values.astype(F32)[:, :, None, :]
    )
    return (mixed / total[..., None]).reshape(rows, -1)


def dequant(levels, scales):
    count, cols = levels.shape
    blocks = scales.shape[0]
    wide = levels.reshape(blocks, count // blocks, cols).astype(F32) * scales[:, None, :]
    return wide.reshape(count, cols).astype(BF)


def chip_index(coords):
    return coords[0] * 16 + coords[1] * 4 + coords[2]


def shift_perm(phase, step):
    pairs = []
    for role in range(2):
        axis = AXES[role][phase]
        for x in range(4):
            for y in range(4):
                for z in range(4):
                    here = [x, y, z]
                    there = list(here)
                    there[axis] = (there[axis] + step) % 4
                    pairs.append((role * 64 + chip_index(here), role * 64 + chip_index(there)))
    return pairs


def send(value, phase, step):
    return lax.ppermute(value, ("role", "shard"), shift_perm(phase, step))


def swap(value):
    return lax.ppermute(value, "role", [(0, 1), (1, 0)])


def ring(value, phase):
    return [value] + [send(value, phase, step) for step in (1, 2, 3)]


def ring_forward(value, phase):
    half = value.shape[0] // 2
    a, b = value[:half], value[half:]
    up_a = send(a, phase, 1)
    down_b = send(b, phase, -1)
    up_b = send(b, phase, 1)
    down_a = send(a, phase, -1)
    far_a = send(up_a, phase, 1)
    far_b = send(down_b, phase, -1)
    cat = lambda p, q: jnp.concatenate([p, q], axis=0)
    return [value, cat(up_a, up_b), cat(far_a, far_b), cat(down_a, down_b)]


def pick(table, index):
    hit = index[:, None] == jnp.arange(table.shape[0], dtype=jnp.int32)[None, :]
    return jnp.sum(jnp.where(hit, table[None, :], 0), axis=1)


def hidden_kernel(o0, o1, o2, o3, r0, r1, r2, r3, low_ref, inv_ref, ids_ref, maps_ref, out_ref):
    own, other = (o0, o1, o2, o3), (r0, r1, r2, r3)
    low = low_ref[...]
    ids = ids_ref[...]
    group = lax.broadcasted_iota(jnp.int32, low.shape, 1) // 16
    rest = ids - group
    acc = jnp.zeros(out_ref.shape, F32)
    for j in range(16):
        parts = [jnp.where(rest == 8 * (2 * j + i), low, 0.0).astype(BF) for i in range(2)]
        lhs = jnp.concatenate(parts, axis=1)
        acc = acc + jnp.dot(lhs, maps_ref[j * 256 : (j + 1) * 256, :], preferred_element_type=F32)
    width = out_ref.shape[1]
    for d3 in range(4):
        for d2 in range(4):
            mine = own[d3][d2 * 32 : (d2 + 1) * 32, :] + other[d2][d3 * 32 : (d3 + 1) * 32, :]
            row = (d3 * 4 + d2) * 32
            inv = inv_ref[row : row + 32, :]
            inv = jnp.concatenate([inv] * (width // 128), axis=1)
            gate = mine[:, :width] * inv + 2.0 * acc[row : row + 32, :]
            up = mine[:, width:] * inv
            out_ref[row : row + 32, :] = (gate / (1.0 + jnp.exp(-gate)) * up).astype(BF)


def make_hidden(own, other, low, inv, ids, maps):
    rows = 512
    width = maps.shape[1]
    return pl.pallas_call(
        hidden_kernel,
        out_shape=jax.ShapeDtypeStruct((rows, width), BF),
        compiler_params=pltpu.CompilerParams(vmem_limit_bytes=40 * 1024 * 1024),
        cost_estimate=pl.CostEstimate(
            flops=2 * rows * 4096 * width, bytes_accessed=7 * 1024 * 1024, transcendentals=rows * width
        ),
    )(*own, *other, low, inv, ids, maps)


def local(
    query,
    fresh_token_keys,
    fresh_token_values,
    stored_keys,
    stored_values,
    slot_cache_length,
    residual,
    prenorm_scale,
    request_cache_slot,
    request_adapter,
    gate_projection_levels,
    gate_group_scales,
    up_projection_levels,
    up_group_scales,
    down_projection_levels,
    down_group_scales,
    adapter_input_maps,
    adapter_gate_maps,
):
    role = lax.axis_index("role")
    shard = lax.axis_index("shard")
    here = (shard // 16, (shard // 4) % 4, shard % 4)
    half = residual.shape[1]
    units = gate_projection_levels.shape[1]
    first = role == 0

    def axis_of(mine, phase):
        a, b = AXES[0][phase], AXES[1][phase]
        return (a, b) if mine else (b, a)

    def by_role(pair, values):
        return jnp.where(first, values[pair[0]], values[pair[1]])

    def position(slot, mine):
        q = slot // 8
        chip = (q // 16, (q // 4) % 4, q % 4)
        total = 0
        for phase in (2, 1, 0):
            pair = axis_of(mine, phase)
            total = total * 4 + (by_role(pair, here) - by_role(pair, chip)) % 4
        return total * 8 + slot % 8

    every = jnp.arange(512, dtype=jnp.int32)
    pos_of_request = position(request_cache_slot, True)
    hit_row = pos_of_request[None, :] == every[:, None]
    adapter_of_row = jnp.sum(jnp.where(hit_row, request_adapter[None, :], 0), axis=1)
    steps = [every // 128, (every // 32) % 4, (every // 8) % 4]
    coords = [None] * 3
    for axis in range(3):
        value = 0
        for place, phase in enumerate((2, 1, 0)):
            pair = axis_of(True, phase)
            mine = jnp.where(first, pair[0], pair[1]) == axis
            value = value + jnp.where(mine, steps[place], 0)
        coords[axis] = (here[axis] + value) % 4
    lane = every % 8
    request = (lane // 4) * 256 + chip_index(coords) * 4 + lane % 4
    slot = pick(request_cache_slot, request)
    pick_mine = (position(slot, True)[:, None] == every[None, :]).astype(BF)
    pick_other = (position(slot, False)[:, None] == every[None, :]).astype(BF)

    gain = prenorm_scale.astype(F32)
    maps = (adapter_input_maps.astype(F32) * gain).astype(BF).reshape(-1, 2 * half)
    maps_keep = lax.dynamic_slice(maps, (0, role * half), (maps.shape[0], half))
    maps_send = lax.dynamic_slice(maps, (0, (1 - role) * half), (maps.shape[0], half))
    maps_chip = jnp.concatenate([maps_keep, swap(maps_send)], axis=0)
    maps_line = jnp.concatenate(ring(maps_chip, 2), axis=0)
    entry = jnp.arange(16, dtype=jnp.int32)
    far = entry // 4
    last = axis_of(True, 2)
    line_coords = [
        jnp.where(jnp.where(first, last[0], last[1]) == axis, (here[axis] - far) % 4, here[axis])
        for axis in range(3)
    ]
    line_role = jnp.where((entry // 2) % 2 == 0, role, 1 - role)
    line_ids = (line_role * 64 + chip_index(line_coords)) * 2 + entry % 2

    attended = attend(
        query,
        fresh_token_keys,
        fresh_token_values,
        stored_keys,
        stored_values,
        slot_cache_length,
        stored_keys.shape[2] // HD,
        HD,
    )
    stream = (residual.astype(F32) + attended).astype(BF)

    line = jnp.concatenate(ring(stream, 0), axis=0)
    plane = jnp.concatenate(ring(line, 1), axis=0)

    def half_weights(levels, scales, which):
        rows = levels.shape[0] // 2
        lev = lax.dynamic_slice(levels, (which * rows, 0), (rows, levels.shape[1]))
        sc = lax.dynamic_slice(scales, (which * (scales.shape[0] // 2), 0), (scales.shape[0] // 2, levels.shape[1]))
        g = lax.dynamic_slice(gain, (which * rows,), (rows,))
        return (dequant(lev, sc).astype(F32) * g[:, None]).astype(BF)

    def both(which):
        return jnp.concatenate(
            [
                half_weights(gate_projection_levels, gate_group_scales, which),
                half_weights(up_projection_levels, up_group_scales, which),
            ],
            axis=1,
        )

    w_send = both(1 - role)
    w_keep = both(role)
    w_recv = swap(w_send)

    def half_down(which):
        lev = lax.dynamic_slice(down_projection_levels, (0, which * half), (units, half))
        sc = lax.dynamic_slice(down_group_scales, (0, which * half), (down_group_scales.shape[0], half))
        return dequant(lev, sc)

    down_recv = swap(half_down(1 - role))
    w_down = jnp.concatenate([half_down(role), down_recv], axis=0)

    blocks = ring_forward(plane, 2)
    own, other = [], []
    for block in blocks:
        other.append(swap(jnp.dot(block, w_recv, preferred_element_type=F32)))
        own.append(jnp.dot(block, w_keep, preferred_element_type=F32))

    products = lax.dot_general(maps_line, plane, (((1,), (1,)), ((), ())), preferred_element_type=F32)
    products = products.reshape(16, 16, 128)
    owned = line_ids[:, None] == adapter_of_row[None, :128]
    low = jnp.sum(jnp.where(owned[:, None, :], products, 0.0), axis=0)
    for phase, size in ((0, 8), (1, 32)):
        parts = ring(low, phase)
        low = parts[0]
        for step in (1, 2, 3):
            wide = parts[step].reshape(16, 128 // (4 * size), 4, size)
            low = low + jnp.roll(wide, step, axis=2).reshape(16, 128)
    wide = plane.astype(F32)
    square = jnp.sum(wide * wide, axis=1)
    extended = jnp.concatenate([low, jnp.broadcast_to(square[None, :], (8, 128))], axis=0)
    extended = jnp.concatenate(ring(extended, 2), axis=1)
    partner = swap(extended).reshape(24, 4, 4, 32).transpose(0, 2, 1, 3).reshape(24, 512)
    extended = extended + partner
    inv = lax.rsqrt(extended[16] / (2 * half) + 1e-05)
    low = (extended[:16] * inv[None, :]).astype(BF).astype(F32)
    low8 = jnp.tile(low.T, (1, 8))
    inv_wide = jnp.broadcast_to(inv[:, None], (512, 128))
    ids_wide = jnp.broadcast_to(adapter_of_row[:, None], (512, 128))

    hidden = make_hidden(own, other, low8, inv_wide, ids_wide, adapter_gate_maps.reshape(-1, units))
    hidden_other = swap(hidden)

    mine = jnp.dot(pick_mine, hidden, preferred_element_type=F32).astype(BF)
    theirs = jnp.dot(pick_other, hidden_other, preferred_element_type=F32).astype(BF)
    both_hidden = jnp.concatenate([mine, theirs], axis=1)

    def product(step):
        return jnp.dot(both_hidden[step * 128 : (step + 1) * 128], w_down, preferred_element_type=F32)

    b2 = product(2).astype(BF)
    far_a = send(b2[:64], 2, 1)
    far_b = send(b2[64:], 2, -1)
    b1 = product(1)
    b3 = product(3)
    near_b = send(b1[64:].astype(BF), 2, 1)
    near_a = send(b3[:64].astype(BF), 2, -1)
    b0 = product(0)
    via_a = send((b1[:64] + far_a.astype(F32)).astype(BF), 2, 1)
    via_b = send((b3[64:] + far_b.astype(F32)).astype(BF), 2, -1)
    sum_a = b0[:64] + via_a.astype(F32) + near_a.astype(F32)
    sum_b = b0[64:] + via_b.astype(F32) + near_b.astype(F32)
    part = [sum_a[:32], sum_a[32:], sum_b[:32], sum_b[32:]]
    for phase, size in ((1, 32), (0, 8)):
        got = [send(part[step].astype(BF), phase, step) for step in (2, 1, 3)]
        total = part[0] + got[0].astype(F32) + got[1].astype(F32) + got[2].astype(F32)
        part = [total[i * (size // 4) : (i + 1) * (size // 4)] for i in range(4)]
    rows8 = pick_mine[:8]
    base = sum(
        jnp.dot(rows8[:, d * 128 : (d + 1) * 128], blocks[d], preferred_element_type=F32) for d in range(4)
    )
    result = (base + total).astype(BF)
    keep = lax.dynamic_slice(result, (role * 4, 0), (4, half))
    got = swap(lax.dynamic_slice(result, ((1 - role) * 4, 0), (4, half)))
    return jnp.concatenate([jnp.where(first, keep, got), jnp.where(first, got, keep)], axis=1)


def solution(mesh):
    return jax.shard_map(
        local,
        mesh=mesh,
        in_specs=(
            P("shard", "role"),
            P("shard", "role"),
            P("shard", "role"),
            P("shard", None, "role"),
            P("shard", None, "role"),
            P("shard"),
            P("shard", "role"),
            P(),
            P(),
            P(),
            P(None, ("role", "shard")),
            P(None, ("role", "shard")),
            P(None, ("role", "shard")),
            P(None, ("role", "shard")),
            P(("role", "shard"), None),
            P(("role", "shard"), None),
            P(("role", "shard"), None, None),
            P(None, None, ("role", "shard")),
        ),
        out_specs=P(("role", "shard"), None),
        check_vma=False,
    )
```

```python
import functools

import jax
import jax.numpy as jnp
from jax import lax
from jax.experimental import pallas as pl
from jax.experimental.pallas import tpu as pltpu
from jax.sharding import PartitionSpec as P

HD = 128
BF = jnp.bfloat16
F32 = jnp.float32
AXES = ((2, 1, 0), (2, 0, 1))


def attend(
    query,
    fresh_token_keys,
    fresh_token_values,
    stored_keys,
    stored_values,
    slot_cache_length,
    kv_heads,
    head_dim,
):
    rows = query.shape[0]
    length = stored_keys.shape[1]
    groups = query.shape[1] // (kv_heads * head_dim)
    queries = query.reshape(rows, kv_heads, groups, head_dim)
    keys = stored_keys.reshape(rows, length, kv_heads, head_dim)
    values = stored_values.reshape(rows, length, kv_heads, head_dim)
    own_keys = fresh_token_keys.reshape(rows, kv_heads, head_dim)
    own_values = fresh_token_values.reshape(rows, kv_heads, head_dim)
    factor = head_dim ** (-0.5)
    scores = jnp.einsum("skgd,slkd->skgl", queries, keys, preferred_element_type=F32) * factor
    valid = jnp.arange(length)[None, :] < slot_cache_length[:, None]
    scores = jnp.where(valid[:, None, None, :], scores, -1e30)
    own = jnp.einsum("skgd,skd->skg", queries, own_keys, preferred_element_type=F32) * factor
    top = jnp.maximum(jnp.max(scores, axis=-1), own)
    weights = jnp.exp(scores - top[..., None])
    own_weight = jnp.exp(own - top)
    total = jnp.sum(weights, axis=-1) + own_weight
    mixed = jnp.einsum("skgl,slkd->skgd", weights.astype(BF), values, preferred_element_type=F32)
    mixed = (
        mixed
        + own_weight.astype(BF).astype(F32)[..., None] * own_values.astype(F32)[:, :, None, :]
    )
    return (mixed / total[..., None]).reshape(rows, -1)


def dequant(levels, scales):
    count, cols = levels.shape
    blocks = scales.shape[0]
    wide = levels.reshape(blocks, count // blocks, cols).astype(F32) * scales[:, None, :]
    return wide.reshape(count, cols).astype(BF)


def weights_kernel(role, gate_ref, gate_scale, up_ref, up_scale, gain_ref, down_ref, down_scale, ready, out_ref, keep_ref, send_ref, token):
    width = gate_ref.shape[1]
    for group in range(gate_ref.shape[0] // 128):
        rows = slice(group * 128, (group + 1) * 128)
        gain = jnp.broadcast_to(gain_ref[0:1, rows], (128, 128)).T
        gain = jnp.concatenate([gain] * (width // 128), axis=1)
        for place, (levels, scales) in enumerate(((gate_ref, gate_scale), (up_ref, up_scale))):
            wide = (levels[rows, :].astype(F32) * scales[group : group + 1, :]).astype(BF)
            out_ref[rows, place * width : (place + 1) * width] = (wide.astype(F32) * gain).astype(BF)
    i = pl.program_id(0)
    half = pl.num_programs(0) // 2
    for ref, here in ((keep_ref, i < half), (send_ref, i >= half)):

        @pl.when(here)
        def _():
            for group in range(down_ref.shape[0] // 128):
                rows = slice(group * 128, (group + 1) * 128)
                ref[rows, :] = (down_ref[rows, :].astype(F32) * down_scale[group : group + 1, :]).astype(BF)

    token[...] = jnp.zeros_like(token)


def make_weights(role, gate, gate_scales, up, up_scales, gain, down, down_scales, ready):
    depth, width = gate.shape
    step = 1024
    count = depth // step
    half = count // 2
    turned = lambda i, r: (i + r[0] * half) % count
    levels = pl.BlockSpec((step, width), lambda i, r: (turned(i, r), 0))
    scales = pl.BlockSpec((step // 128, width), lambda i, r: (turned(i, r), 0))
    across = lambda rows: pl.BlockSpec((rows, step), lambda i, r: (0, turned(i, r)))
    return pl.pallas_call(
        weights_kernel,
        out_shape=[
            jax.ShapeDtypeStruct((depth, 2 * width), BF),
            jax.ShapeDtypeStruct((width, depth // 2), BF),
            jax.ShapeDtypeStruct((width, depth // 2), BF),
            jax.ShapeDtypeStruct((16, 128), BF),
        ],
        grid_spec=pltpu.PrefetchScalarGridSpec(
            num_scalar_prefetch=1,
            grid=(count,),
            in_specs=[levels, scales, levels, scales, across(1), across(width), across(down_scales.shape[0]), pl.BlockSpec((8, 128), lambda i, r: (0, 0))],
            out_specs=[
                pl.BlockSpec((step, 2 * width), lambda i, r: (i, 0)),
                pl.BlockSpec((width, step), lambda i, r: (0, jnp.minimum(i, half - 1))),
                pl.BlockSpec((width, step), lambda i, r: (0, jnp.maximum(i - half, 0))),
                pl.BlockSpec((16, 128), lambda i, r: (0, 0)),
            ],
        ),
        compiler_params=pltpu.CompilerParams(vmem_limit_bytes=48 * 1024 * 1024),
        cost_estimate=pl.CostEstimate(flops=12 * depth * width, bytes_accessed=12 * depth * width, transcendentals=0),
    )(role.reshape(1), gate, gate_scales, up, up_scales, gain, down, down_scales, ready)


def chip_index(coords):
    return coords[0] * 16 + coords[1] * 4 + coords[2]


def shift_perm(phase, step):
    pairs = []
    for role in range(2):
        axis = AXES[role][phase]
        for x in range(4):
            for y in range(4):
                for z in range(4):
                    here = [x, y, z]
                    there = list(here)
                    there[axis] = (there[axis] + step) % 4
                    pairs.append((role * 64 + chip_index(here), role * 64 + chip_index(there)))
    return pairs


def send(value, phase, step):
    return lax.ppermute(value, ("role", "shard"), shift_perm(phase, step))


def swap(value):
    return lax.ppermute(value, "role", [(0, 1), (1, 0)])


def plane_groups():
    groups = []
    for role in range(2):
        across, last = AXES[role][1], AXES[role][2]
        for fixed in range(4):
            group = []
            for z in range(4):
                for w in range(4):
                    coords = [0, 0, z]
                    coords[across], coords[last] = w, fixed
                    group.append(role * 64 + chip_index(coords))
            groups.append(group)
    return groups


def exchange(value):
    return lax.all_to_all(value, ("role", "shard"), 0, 0, axis_index_groups=plane_groups())


def ring(value, phase):
    return [value] + [send(value, phase, step) for step in (1, 2, 3)]


def after(value, *others):
    for other in others:
        cut = other[tuple(slice(0, min(n, m)) for n, m in zip(value.shape, other.shape))]
        zero = (cut * 0).astype(value.dtype)
        value = value + jnp.pad(zero, [(0, n - m) for n, m in zip(value.shape, zero.shape)])
    return value


def pick(table, index):
    hit = index[:, None] == jnp.arange(table.shape[0], dtype=jnp.int32)[None, :]
    return jnp.sum(jnp.where(hit, table[None, :], 0), axis=1)


def low_kernel(ids, x0, x1, x3, near_ref, far_ref, gain_ref, rows_ref, out_ref):
    gain = gain_ref[...].astype(F32)
    near = (near_ref[...].astype(F32) * gain).astype(BF)
    far = (far_ref[...].astype(F32) * gain).astype(BF)
    turn = (((1,), (1,)), ((), ()))
    parts = []
    for place, x in enumerate((x0, x1, x3)):
        block = x[...]
        rows = rows_ref[0:1, place * 128 : (place + 1) * 128]
        total = jnp.zeros((16, 128), F32)
        for base, table in ((0, near), (4, far)):
            if base == 4 and place > 0:
                continue
            got = lax.dot_general(table, block, turn, preferred_element_type=F32)
            for entry in range(4):
                total = total + jnp.where(rows == ids[base + entry], got[entry * 16 : (entry + 1) * 16, :], 0.0)
        parts.append(total)
    low = jnp.concatenate(parts, axis=1)
    for copy in range(16):
        out_ref[copy] = low


def make_low(ids, blocks, near, far, gain, rows):
    whole = pl.BlockSpec(memory_space=pltpu.VMEM)
    return pl.pallas_call(
        low_kernel,
        out_shape=jax.ShapeDtypeStruct((16, 16, 384), F32),
        in_specs=[pl.BlockSpec(memory_space=pltpu.SMEM)] + [whole] * 7,
        out_specs=whole,
        compiler_params=pltpu.CompilerParams(vmem_limit_bytes=48 * 1024 * 1024),
        cost_estimate=pl.CostEstimate(flops=2 * 256 * 128 * 4096, bytes_accessed=5 * 1024 * 1024, transcendentals=0),
    )(ids, *blocks, near, far, gain, rows)


def products_kernel(count, *refs):
    mine, others = refs[:count], refs[count : 2 * count]
    w_mine, w_other, pick_ref, own, other, own_sq, other_sq, base = refs[2 * count :]

    @pl.when(pl.program_id(0) == 0)
    def _():
        own[...] = jnp.zeros_like(own)
        other[...] = jnp.zeros_like(other)
        own_sq[...] = jnp.zeros_like(own_sq)
        other_sq[...] = jnp.zeros_like(other_sq)

    for parts, weights, out, square in ((mine, w_mine, own, own_sq), (others, w_other, other, other_sq)):
        x = jnp.concatenate([part[...] for part in parts], axis=0)
        out[...] += jnp.dot(x, weights[...], preferred_element_type=F32)
        wide = x.astype(F32)
        wide = wide * wide
        square[...] += sum(wide[:, i * 128 : (i + 1) * 128] for i in range(wide.shape[1] // 128))
        if out is own:
            base[...] = jnp.dot(pick_ref[...], x, preferred_element_type=F32)


def make_products(mine, others, weights, pick):
    step = 1024
    depth, width = weights.shape[0] // 2, weights.shape[1]
    count = len(mine)
    rows = 128 * count
    x_spec = pl.BlockSpec((128, step), lambda k: (0, k))
    mine_spec = pl.BlockSpec((step, width), lambda k: (k, 0))
    other_spec = pl.BlockSpec((step, width), lambda k: (k + depth // step, 0))
    fixed = lambda *shape: pl.BlockSpec(shape, lambda k: (0, 0))
    return pl.pallas_call(
        functools.partial(products_kernel, count),
        out_shape=[
            jax.ShapeDtypeStruct((rows, width), F32),
            jax.ShapeDtypeStruct((rows, width), F32),
            jax.ShapeDtypeStruct((rows, 128), F32),
            jax.ShapeDtypeStruct((rows, 128), F32),
            jax.ShapeDtypeStruct((8, depth), F32),
        ],
        grid=(depth // step,),
        in_specs=[x_spec] * (2 * count) + [mine_spec, other_spec, fixed(8, rows)],
        out_specs=[fixed(rows, width), fixed(rows, width), fixed(rows, 128), fixed(rows, 128), pl.BlockSpec((8, step), lambda k: (0, k))],
        compiler_params=pltpu.CompilerParams(vmem_limit_bytes=48 * 1024 * 1024),
        cost_estimate=pl.CostEstimate(
            flops=4 * rows * depth * width, bytes_accessed=(12 + 2 * count) * 1024 * 1024, transcendentals=0
        ),
    )(*mine, *others, weights, weights, pick)


def hidden_kernel(place, own_a, other_a, own_sq_a, other_sq_a, own_b, other_b, own_sq_b, other_sq_b, low_ref, low_other, ids_ref, pos_mine, pos_other, maps_ref, out_ref, out_other, low_got, sq, hidden, other, other_sq):
    def there(d, z, w):
        row = ((place[1] - w) & 3) * 128 + z * 32 + ((place[0] - d) & 3) * 8
        return pl.ds(pl.multiple_of(row, 8), 8)

    for part_a, part_b, into in ((other_a, other_b, other), (other_sq_a, other_sq_b, other_sq)):
        into[0:256, :] = part_a[0:256, :]
        into[256:384, :] = part_b[...]
        into[384:512, :] = part_a[256:384, :]
    source = lambda d: (d == 2, (0, 128, 0, 256)[d])
    fill = jnp.zeros((112, 512), F32)
    low_got[...] = jnp.concatenate([low_other[...], fill], axis=0).T
    low_mine = jnp.concatenate([low_ref[...], fill], axis=0).T
    parts = []
    for d in range(4):
        for z in range(4):
            for w in range(4):
                row = d * 128 + z * 32 + w * 8
                second, start = source(d)
                mine = (own_sq_b if second else own_sq_a)[start + z * 32 + w * 8 : start + z * 32 + w * 8 + 8, :]
                sq[row : row + 8, :] = mine + other_sq[there(d, z, w), :]
                parts.append(low_got[there(d, z, w), :])
    inv = lax.rsqrt(jnp.sum(sq[...], axis=1, keepdims=True) / 8192.0 + 1e-05)
    total = low_mine + jnp.concatenate(parts, axis=0)
    column = lax.broadcasted_iota(jnp.int32, (128, 128), 0)
    lane = lax.broadcasted_iota(jnp.int32, (128, 128), 1)
    spread = jnp.where(column == lane % 16, 1.0, 0.0).astype(BF)
    low = jnp.dot((total * inv).astype(BF), spread, preferred_element_type=F32)
    inv = jnp.broadcast_to(inv, (512, 128))
    lane = lax.broadcasted_iota(jnp.int32, (512, 128), 1)
    rest = ids_ref[...] - lane // 16
    acc = jnp.zeros(out_ref.shape, F32)
    for j in range(16):
        sides = [jnp.where(rest == 8 * (2 * j + i), low, 0.0).astype(BF) for i in range(2)]
        lhs = jnp.concatenate(sides, axis=1)
        acc = acc + jnp.dot(lhs, maps_ref[j * 256 : (j + 1) * 256, :], preferred_element_type=F32)
    width = out_ref.shape[1]
    for d in range(4):
        for z in range(4):
            for v in range(2):
                row = d * 128 + z * 32 + v * 16
                sums = [other[there(d, z, w), :] for w in (2 * v, 2 * v + 1)]
                second, start = source(d)
                start = start + z * 32 + v * 16
                both = (own_b if second else own_a)[start : start + 16, :] + jnp.concatenate(sums, axis=0)
                scale = jnp.concatenate([inv[row : row + 16, :]] * (width // 128), axis=1)
                gate = both[:, :width] * scale + 2.0 * acc[row : row + 16, :]
                up = both[:, width:] * scale
                hidden[row : row + 16, :] = (gate / (1.0 + jnp.exp(-gate)) * up).astype(BF)
    value = hidden[...]
    for pos_ref, out in ((pos_mine, out_ref), (pos_other, out_other)):
        pos = pos_ref[...]
        pick = jnp.concatenate([jnp.where(pos == lane + 128 * i, 1.0, 0.0).astype(BF) for i in range(4)], axis=1)
        out[...] = jnp.dot(pick, value, preferred_element_type=F32).astype(BF)


def make_hidden(place, first, second, low, low_other, ids, pos_mine, pos_other, maps):
    rows = 512
    width = maps.shape[1]
    whole = pl.BlockSpec(memory_space=pltpu.VMEM)
    return pl.pallas_call(
        hidden_kernel,
        out_shape=[jax.ShapeDtypeStruct((rows, width), BF)] * 2,
        in_specs=[pl.BlockSpec(memory_space=pltpu.SMEM)] + [whole] * 14,
        out_specs=[whole] * 2,
        scratch_shapes=[pltpu.VMEM((rows, 128), F32), pltpu.VMEM((rows, 128), F32), pltpu.VMEM((rows, width), BF), pltpu.VMEM((rows, 2 * width), F32), pltpu.VMEM((rows, 128), F32)],
        compiler_params=pltpu.CompilerParams(vmem_limit_bytes=48 * 1024 * 1024),
        cost_estimate=pl.CostEstimate(
            flops=2 * rows * 4096 * width, bytes_accessed=6 * 1024 * 1024, transcendentals=rows * width
        ),
    )(place, *first, *second, low, low_other, ids, pos_mine, pos_other, maps)


def down_kernel(mine_ref, other_ref, keep_ref, recv_ref, o0, o1, o2, o3):
    rows = jnp.concatenate([mine_ref[...], other_ref[...]], axis=1)
    weights = jnp.concatenate([keep_ref[...], recv_ref[...]], axis=0)
    total = jnp.dot(rows, weights, preferred_element_type=F32)
    for step, out in enumerate((o0, o1, o2, o3)):
        out[...] = total[step * 128 : (step + 1) * 128].astype(out.dtype)


def make_down(mine, other, keep, recv):
    rows, width = mine.shape
    columns = keep.shape[1]
    step = 1024
    whole = lambda x: pl.BlockSpec(x.shape, lambda i: (0, 0))
    tile = lambda n: pl.BlockSpec((n, step), lambda i: (0, i))
    return pl.pallas_call(
        down_kernel,
        out_shape=[jax.ShapeDtypeStruct((rows // 4, columns), F32 if d == 0 else BF) for d in range(4)],
        grid=(columns // step,),
        in_specs=[whole(mine), whole(other), tile(width), tile(width)],
        out_specs=[tile(rows // 4)] * 4,
        compiler_params=pltpu.CompilerParams(vmem_limit_bytes=48 * 1024 * 1024),
        cost_estimate=pl.CostEstimate(
            flops=4 * rows * width * columns, bytes_accessed=9 * 1024 * 1024, transcendentals=0
        ),
    )(mine, other, keep, recv)


def local(
    query,
    fresh_token_keys,
    fresh_token_values,
    stored_keys,
    stored_values,
    slot_cache_length,
    residual,
    prenorm_scale,
    request_cache_slot,
    request_adapter,
    gate_projection_levels,
    gate_group_scales,
    up_projection_levels,
    up_group_scales,
    down_projection_levels,
    down_group_scales,
    adapter_input_maps,
    adapter_gate_maps,
):
    role = lax.axis_index("role")
    shard = lax.axis_index("shard")
    here = (shard // 16, (shard // 4) % 4, shard % 4)
    half = residual.shape[1]
    units = gate_projection_levels.shape[1]
    first = role == 0

    def axis_of(mine, phase):
        a, b = AXES[0][phase], AXES[1][phase]
        return (a, b) if mine else (b, a)

    def by_role(pair, values):
        return jnp.where(first, values[pair[0]], values[pair[1]])

    def position(slot, mine):
        q = slot // 8
        chip = (q // 16, (q // 4) % 4, q % 4)
        last, across = axis_of(mine, 2), axis_of(mine, 1)
        total = (by_role(last, here) - by_role(last, chip)) % 4
        return (total * 16 + chip[2] * 4 + by_role(across, chip)) * 8 + slot % 8

    every = jnp.arange(512, dtype=jnp.int32)
    pos_of_request = position(request_cache_slot, True)
    hit_row = pos_of_request[None, :] == every[:, None]
    adapter_of_row = jnp.sum(jnp.where(hit_row, request_adapter[None, :], 0), axis=1)
    def request_slots(mine):
        z, w = (every // 32) % 4, (every // 8) % 4
        far = (by_role(axis_of(mine, 2), here) + every // 128) % 4
        swapped = first if mine else jnp.logical_not(first)
        chip = chip_index((jnp.where(swapped, far, w), jnp.where(swapped, w, far), z))
        lane = every % 8
        return pick(request_cache_slot, (lane // 4) * 256 + chip * 4 + lane % 4)

    slots = request_slots(True)
    pos_mine = jnp.broadcast_to(position(slots, True)[:, None], (512, 128))
    pos_other = jnp.broadcast_to(position(request_slots(False), True)[:, None], (512, 128))
    own_place = here[2] * 4 + by_role(axis_of(True, 1), here)
    own_pos = position(lax.dynamic_slice(slots, (own_place * 8,), (8,)), True)
    own_pick = (own_pos[:, None] == every[None, :]).astype(BF)

    gain = prenorm_scale.astype(F32)
    maps_raw = adapter_input_maps.reshape(-1, 2 * half)
    maps_keep = lax.dynamic_slice(maps_raw, (0, role * half), (maps_raw.shape[0], half))
    maps_send = lax.dynamic_slice(maps_raw, (0, (1 - role) * half), (maps_raw.shape[0], half))
    maps_near = jnp.concatenate([maps_keep, swap(maps_send)], axis=0)
    last = axis_of(True, 2)

    def adapters_at(step, of_role):
        mine = [jnp.where(first, last[0], last[1]) == axis for axis in range(3)]
        chip = chip_index([jnp.where(m, (c + step) % 4, c) for m, c in zip(mine, here)])
        return (of_role * 64 + chip) * 2 + jnp.arange(2, dtype=jnp.int32)

    ids = jnp.concatenate([adapters_at(step, of) for step in (0, 2) for of in (role, 1 - role)])

    attended = attend(
        query,
        fresh_token_keys,
        fresh_token_values,
        stored_keys,
        stored_values,
        slot_cache_length,
        stored_keys.shape[2] // HD,
        HD,
    )
    stream = (residual.astype(F32) + attended).astype(BF)

    weights, down_keep, down_send, token = make_weights(
        role,
        gate_projection_levels,
        gate_group_scales,
        up_projection_levels,
        up_group_scales,
        gain.reshape(1, -1),
        down_projection_levels,
        down_group_scales,
        stream[:, :128],
    )
    maps_far = send(after(maps_near, stream), 2, 2)

    plane = exchange(jnp.broadcast_to(stream[None], (16,) + stream.shape)).reshape(128, half)
    plane = after(plane, token, maps_far)
    down_recv = swap(down_send)

    up = send(plane, 2, 1)
    down = send(plane, 2, -1)
    far_block = send(up, 2, 1)
    blocks = (plane, up, far_block, down)
    gain_half = lax.dynamic_slice(gain, (role * half,), (half,)).reshape(1, half)
    low_rows = jnp.concatenate([adapter_of_row[:256], adapter_of_row[384:]]).reshape(1, 384)
    low = make_low(ids, (plane, up, down), maps_near, maps_far, gain_half, low_rows)
    low = jnp.sum(exchange(low), axis=0)
    others = [swap(block) for block in (plane, up, down)]
    pick_first = jnp.concatenate([own_pick[:, :256], own_pick[:, 384:]], axis=1)
    *early, base = make_products((plane, up, down), others, weights, after(pick_first, low))
    far_other = swap(after(far_block, early[0]))
    *late, base_far = make_products((far_block,), (far_other,), weights, own_pick[:, 256:384])
    got = ring(low, 2)
    column = {0: 0, 1: 128, 3: 256}
    sums = []
    for d in range(4):
        terms = [got[step][:, column[(d - step) % 4] :][:, :128] for step in range(4) if (d - step) % 4 != 2]
        sums.append(sum(terms[1:], terms[0]))
    low = jnp.concatenate(sums, axis=1)
    low_other = swap(low)

    ids_wide = jnp.broadcast_to(adapter_of_row[:, None], (512, 128))
    place = jnp.stack([by_role(axis_of(True, 2), here), by_role(axis_of(False, 2), here)])
    hidden, hidden_send = make_hidden(
        place, early, late, low, low_other, ids_wide, pos_mine, pos_other, adapter_gate_maps.reshape(-1, units)
    )
    hidden_other = swap(hidden_send)

    pieces = make_down(hidden, hidden_other, down_keep, down_recv)
    got = [send(pieces[step], 2, step) for step in (2, 1, 3)]
    total = pieces[0] + got[0].astype(F32) + got[1].astype(F32) + got[2].astype(F32)
    part = total.astype(BF).reshape(16, 8, half)
    total = jnp.sum(exchange(part).astype(F32), axis=0)
    result = (base + base_far + total).astype(BF)
    keep = lax.dynamic_slice(result, (role * 4, 0), (4, half))
    got = swap(lax.dynamic_slice(result, ((1 - role) * 4, 0), (4, half)))
    return jnp.concatenate([jnp.where(first, keep, got), jnp.where(first, got, keep)], axis=1)


def solution(mesh):
    return jax.shard_map(
        local,
        mesh=mesh,
        in_specs=(
            P("shard", "role"),
            P("shard", "role"),
            P("shard", "role"),
            P("shard", None, "role"),
            P("shard", None, "role"),
            P("shard"),
            P("shard", "role"),
            P(),
            P(),
            P(),
            P(None, ("role", "shard")),
            P(None, ("role", "shard")),
            P(None, ("role", "shard")),
            P(None, ("role", "shard")),
            P(("role", "shard"), None),
            P(("role", "shard"), None),
            P(("role", "shard"), None, None),
            P(None, None, ("role", "shard")),
        ),
        out_specs=P(("role", "shard"), None),
        check_vma=False,
    )
```

```python
import functools

import jax
import jax.numpy as jnp
from jax import lax
from jax.experimental import pallas as pl
from jax.experimental.pallas import tpu as pltpu
from jax.sharding import PartitionSpec as P

HD = 128
BF = jnp.bfloat16
F32 = jnp.float32
AXES = ((2, 1, 0), (2, 0, 1))


def attend(
    query,
    fresh_token_keys,
    fresh_token_values,
    stored_keys,
    stored_values,
    slot_cache_length,
    kv_heads,
    head_dim,
):
    rows = query.shape[0]
    length = stored_keys.shape[1]
    groups = query.shape[1] // (kv_heads * head_dim)
    queries = query.reshape(rows, kv_heads, groups, head_dim)
    keys = stored_keys.reshape(rows, length, kv_heads, head_dim)
    values = stored_values.reshape(rows, length, kv_heads, head_dim)
    own_keys = fresh_token_keys.reshape(rows, kv_heads, head_dim)
    own_values = fresh_token_values.reshape(rows, kv_heads, head_dim)
    factor = head_dim ** (-0.5)
    scores = jnp.einsum("skgd,slkd->skgl", queries, keys, preferred_element_type=F32) * factor
    valid = jnp.arange(length)[None, :] < slot_cache_length[:, None]
    scores = jnp.where(valid[:, None, None, :], scores, -1e30)
    own = jnp.einsum("skgd,skd->skg", queries, own_keys, preferred_element_type=F32) * factor
    top = jnp.maximum(jnp.max(scores, axis=-1), own)
    weights = jnp.exp(scores - top[..., None])
    own_weight = jnp.exp(own - top)
    total = jnp.sum(weights, axis=-1) + own_weight
    mixed = jnp.einsum("skgl,slkd->skgd", weights.astype(BF), values, preferred_element_type=F32)
    mixed = (
        mixed
        + own_weight.astype(BF).astype(F32)[..., None] * own_values.astype(F32)[:, :, None, :]
    )
    return (mixed / total[..., None]).reshape(rows, -1)


def dequant(levels, scales):
    count, cols = levels.shape
    blocks = scales.shape[0]
    wide = levels.reshape(blocks, count // blocks, cols).astype(F32) * scales[:, None, :]
    return wide.reshape(count, cols).astype(BF)


def weights_kernel(role, gate_ref, gate_scale, up_ref, up_scale, gain_ref, down_ref, down_scale, ready, out_ref, keep_ref, send_ref, token):
    width = gate_ref.shape[1]
    for group in range(gate_ref.shape[0] // 128):
        rows = slice(group * 128, (group + 1) * 128)
        gain = jnp.broadcast_to(gain_ref[0:1, rows], (128, 128)).T
        gain = jnp.concatenate([gain] * (width // 128), axis=1)
        for place, (levels, scales) in enumerate(((gate_ref, gate_scale), (up_ref, up_scale))):
            wide = (levels[rows, :].astype(F32) * scales[group : group + 1, :]).astype(BF)
            out_ref[rows, place * width : (place + 1) * width] = (wide.astype(F32) * gain).astype(BF)
    i = pl.program_id(0)
    half = pl.num_programs(0) // 2
    for ref, here in ((keep_ref, i < half), (send_ref, i >= half)):

        @pl.when(here)
        def _():
            for group in range(down_ref.shape[0] // 128):
                rows = slice(group * 128, (group + 1) * 128)
                ref[rows, :] = (down_ref[rows, :].astype(F32) * down_scale[group : group + 1, :]).astype(BF)

    token[...] = jnp.zeros_like(token)


def make_weights(role, gate, gate_scales, up, up_scales, gain, down, down_scales, ready):
    depth, width = gate.shape
    step = 1024
    count = depth // step
    half = count // 2
    turned = lambda i, r: (i + r[0] * half) % count
    levels = pl.BlockSpec((step, width), lambda i, r: (turned(i, r), 0))
    scales = pl.BlockSpec((step // 128, width), lambda i, r: (turned(i, r), 0))
    across = lambda rows: pl.BlockSpec((rows, step), lambda i, r: (0, turned(i, r)))
    return pl.pallas_call(
        weights_kernel,
        out_shape=[
            jax.ShapeDtypeStruct((depth, 2 * width), BF),
            jax.ShapeDtypeStruct((width, depth // 2), BF),
            jax.ShapeDtypeStruct((width, depth // 2), BF),
            jax.ShapeDtypeStruct((16, 128), BF),
        ],
        grid_spec=pltpu.PrefetchScalarGridSpec(
            num_scalar_prefetch=1,
            grid=(count,),
            in_specs=[levels, scales, levels, scales, across(1), across(width), across(down_scales.shape[0]), pl.BlockSpec((8, 128), lambda i, r: (0, 0))],
            out_specs=[
                pl.BlockSpec((step, 2 * width), lambda i, r: (i, 0)),
                pl.BlockSpec((width, step), lambda i, r: (0, jnp.minimum(i, half - 1))),
                pl.BlockSpec((width, step), lambda i, r: (0, jnp.maximum(i - half, 0))),
                pl.BlockSpec((16, 128), lambda i, r: (0, 0)),
            ],
        ),
        compiler_params=pltpu.CompilerParams(vmem_limit_bytes=48 * 1024 * 1024),
        cost_estimate=pl.CostEstimate(flops=12 * depth * width, bytes_accessed=12 * depth * width, transcendentals=0),
    )(role.reshape(1), gate, gate_scales, up, up_scales, gain, down, down_scales, ready)


def chip_index(coords):
    return coords[0] * 16 + coords[1] * 4 + coords[2]


def shift_perm(phase, step):
    pairs = []
    for role in range(2):
        axis = AXES[role][phase]
        for x in range(4):
            for y in range(4):
                for z in range(4):
                    here = [x, y, z]
                    there = list(here)
                    there[axis] = (there[axis] + step) % 4
                    pairs.append((role * 64 + chip_index(here), role * 64 + chip_index(there)))
    return pairs


def send(value, phase, step):
    return lax.ppermute(value, ("role", "shard"), shift_perm(phase, step))


def swap(value):
    return lax.ppermute(value, "role", [(0, 1), (1, 0)])


def plane_groups():
    groups = []
    for role in range(2):
        across, last = AXES[role][1], AXES[role][2]
        for fixed in range(4):
            group = []
            for z in range(4):
                for w in range(4):
                    coords = [0, 0, z]
                    coords[across], coords[last] = w, fixed
                    group.append(role * 64 + chip_index(coords))
            groups.append(group)
    return groups


def exchange(value):
    return lax.all_to_all(value, ("role", "shard"), 0, 0, axis_index_groups=plane_groups())


def ring(value, phase):
    return [value] + [send(value, phase, step) for step in (1, 2, 3)]


def after(value, *others):
    for other in others:
        cut = other[tuple(slice(0, min(n, m)) for n, m in zip(value.shape, other.shape))]
        zero = (cut * 0).astype(value.dtype)
        value = value + jnp.pad(zero, [(0, n - m) for n, m in zip(value.shape, zero.shape)])
    return value


def pick(table, index):
    hit = index[:, None] == jnp.arange(table.shape[0], dtype=jnp.int32)[None, :]
    return jnp.sum(jnp.where(hit, table[None, :], 0), axis=1)


def low_kernel(ids, x0, x1, x3, near_ref, far_ref, gain_ref, rows_ref, out_ref):
    gain = gain_ref[...].astype(F32)
    near = (near_ref[...].astype(F32) * gain).astype(BF)
    far = (far_ref[...].astype(F32) * gain).astype(BF)
    turn = (((1,), (1,)), ((), ()))
    parts = []
    for place, x in enumerate((x0, x1, x3)):
        block = x[...]
        rows = rows_ref[0:1, place * 128 : (place + 1) * 128]
        total = jnp.zeros((16, 128), F32)
        for base, table in ((0, near), (4, far)):
            if base == 4 and place > 0:
                continue
            got = lax.dot_general(table, block, turn, preferred_element_type=F32)
            for entry in range(4):
                total = total + jnp.where(rows == ids[base + entry], got[entry * 16 : (entry + 1) * 16, :], 0.0)
        parts.append(total)
    low = jnp.concatenate(parts, axis=1)
    for copy in range(16):
        out_ref[copy] = low


def make_low(ids, blocks, near, far, gain, rows):
    whole = pl.BlockSpec(memory_space=pltpu.VMEM)
    return pl.pallas_call(
        low_kernel,
        out_shape=jax.ShapeDtypeStruct((16, 16, 384), F32),
        in_specs=[pl.BlockSpec(memory_space=pltpu.SMEM)] + [whole] * 7,
        out_specs=whole,
        compiler_params=pltpu.CompilerParams(vmem_limit_bytes=48 * 1024 * 1024),
        cost_estimate=pl.CostEstimate(flops=2 * 256 * 128 * 4096, bytes_accessed=5 * 1024 * 1024, transcendentals=0),
    )(ids, *blocks, near, far, gain, rows)


def products_kernel(count, *refs):
    mine, others = refs[:count], refs[count : 2 * count]
    w_mine, w_other, pick_ref, own, other, own_sq, other_sq, base = refs[2 * count :]

    @pl.when(pl.program_id(0) == 0)
    def _():
        own[...] = jnp.zeros_like(own)
        other[...] = jnp.zeros_like(other)
        own_sq[...] = jnp.zeros_like(own_sq)
        other_sq[...] = jnp.zeros_like(other_sq)

    for parts, weights, out, square in ((mine, w_mine, own, own_sq), (others, w_other, other, other_sq)):
        x = jnp.concatenate([part[...] for part in parts], axis=0)
        out[...] += jnp.dot(x, weights[...], preferred_element_type=F32)
        wide = x.astype(F32)
        wide = wide * wide
        square[...] += sum(wide[:, i * 128 : (i + 1) * 128] for i in range(wide.shape[1] // 128))
        if out is own:
            base[...] = jnp.dot(pick_ref[...], x, preferred_element_type=F32)


def make_products(mine, others, weights, pick):
    step = 1024
    depth, width = weights.shape[0] // 2, weights.shape[1]
    count = len(mine)
    rows = 128 * count
    x_spec = pl.BlockSpec((128, step), lambda k: (0, k))
    mine_spec = pl.BlockSpec((step, width), lambda k: (k, 0))
    other_spec = pl.BlockSpec((step, width), lambda k: (k + depth // step, 0))
    fixed = lambda *shape: pl.BlockSpec(shape, lambda k: (0, 0))
    return pl.pallas_call(
        functools.partial(products_kernel, count),
        out_shape=[
            jax.ShapeDtypeStruct((rows, width), F32),
            jax.ShapeDtypeStruct((rows, width), F32),
            jax.ShapeDtypeStruct((rows, 128), F32),
            jax.ShapeDtypeStruct((rows, 128), F32),
            jax.ShapeDtypeStruct((8, depth), F32),
        ],
        grid=(depth // step,),
        in_specs=[x_spec] * (2 * count) + [mine_spec, other_spec, fixed(8, rows)],
        out_specs=[fixed(rows, width), fixed(rows, width), fixed(rows, 128), fixed(rows, 128), pl.BlockSpec((8, step), lambda k: (0, k))],
        compiler_params=pltpu.CompilerParams(vmem_limit_bytes=48 * 1024 * 1024),
        cost_estimate=pl.CostEstimate(
            flops=4 * rows * depth * width, bytes_accessed=(12 + 2 * count) * 1024 * 1024, transcendentals=0
        ),
    )(*mine, *others, weights, weights, pick)


def hidden_kernel(place, own_a, other_a, own_sq_a, other_sq_a, own_b, other_b, own_sq_b, other_sq_b, low_ref, low_other, ids_ref, pos_mine, pos_other, maps_ref, out_ref, out_other, low_got, sq, hidden, other, other_sq):
    def there(d, z, w):
        row = ((place[1] - w) & 3) * 128 + z * 32 + ((place[0] - d) & 3) * 8
        return pl.ds(pl.multiple_of(row, 8), 8)

    for part_a, part_b, into in ((other_a, other_b, other), (other_sq_a, other_sq_b, other_sq)):
        into[0:256, :] = part_a[0:256, :]
        into[256:384, :] = part_b[...]
        into[384:512, :] = part_a[256:384, :]
    source = lambda d: (d == 2, (0, 128, 0, 256)[d])
    fill = jnp.zeros((112, 512), F32)
    low_got[...] = jnp.concatenate([low_other[...], fill], axis=0).T
    low_mine = jnp.concatenate([low_ref[...], fill], axis=0).T
    parts = []
    for d in range(4):
        for z in range(4):
            for w in range(4):
                row = d * 128 + z * 32 + w * 8
                second, start = source(d)
                mine = (own_sq_b if second else own_sq_a)[start + z * 32 + w * 8 : start + z * 32 + w * 8 + 8, :]
                sq[row : row + 8, :] = mine + other_sq[there(d, z, w), :]
                parts.append(low_got[there(d, z, w), :])
    inv = lax.rsqrt(jnp.sum(sq[...], axis=1, keepdims=True) / 8192.0 + 1e-05)
    total = low_mine + jnp.concatenate(parts, axis=0)
    column = lax.broadcasted_iota(jnp.int32, (128, 128), 0)
    lane = lax.broadcasted_iota(jnp.int32, (128, 128), 1)
    spread = jnp.where(column == lane % 16, 1.0, 0.0).astype(BF)
    low = jnp.dot((total * inv).astype(BF), spread, preferred_element_type=F32)
    inv = jnp.broadcast_to(inv, (512, 128))
    lane = lax.broadcasted_iota(jnp.int32, (512, 128), 1)
    rest = ids_ref[...] - lane // 16
    acc = jnp.zeros(out_ref.shape, F32)
    for j in range(16):
        sides = [jnp.where(rest == 8 * (2 * j + i), low, 0.0).astype(BF) for i in range(2)]
        lhs = jnp.concatenate(sides, axis=1)
        acc = acc + jnp.dot(lhs, maps_ref[j * 256 : (j + 1) * 256, :], preferred_element_type=F32)
    width = out_ref.shape[1]
    for d in range(4):
        for z in range(4):
            for v in range(2):
                row = d * 128 + z * 32 + v * 16
                sums = [other[there(d, z, w), :] for w in (2 * v, 2 * v + 1)]
                second, start = source(d)
                start = start + z * 32 + v * 16
                both = (own_b if second else own_a)[start : start + 16, :] + jnp.concatenate(sums, axis=0)
                scale = jnp.concatenate([inv[row : row + 16, :]] * (width // 128), axis=1)
                gate = both[:, :width] * scale + 2.0 * acc[row : row + 16, :]
                up = both[:, width:] * scale
                hidden[row : row + 16, :] = (gate / (1.0 + jnp.exp(-gate)) * up).astype(BF)
    value = hidden[...]
    for pos_ref, out in ((pos_mine, out_ref), (pos_other, out_other)):
        pos = pos_ref[...]
        pick = jnp.concatenate([jnp.where(pos == lane + 128 * i, 1.0, 0.0).astype(BF) for i in range(4)], axis=1)
        out[...] = jnp.dot(pick, value, preferred_element_type=F32).astype(BF)


def make_hidden(place, first, second, low, low_other, ids, pos_mine, pos_other, maps):
    rows = 512
    width = maps.shape[1]
    whole = pl.BlockSpec(memory_space=pltpu.VMEM)
    return pl.pallas_call(
        hidden_kernel,
        out_shape=[jax.ShapeDtypeStruct((rows, width), BF)] * 2,
        in_specs=[pl.BlockSpec(memory_space=pltpu.SMEM)] + [whole] * 14,
        out_specs=[whole] * 2,
        scratch_shapes=[pltpu.VMEM((rows, 128), F32), pltpu.VMEM((rows, 128), F32), pltpu.VMEM((rows, width), BF), pltpu.VMEM((rows, 2 * width), F32), pltpu.VMEM((rows, 128), F32)],
        compiler_params=pltpu.CompilerParams(vmem_limit_bytes=48 * 1024 * 1024),
        cost_estimate=pl.CostEstimate(
            flops=2 * rows * 4096 * width, bytes_accessed=6 * 1024 * 1024, transcendentals=rows * width
        ),
    )(place, *first, *second, low, low_other, ids, pos_mine, pos_other, maps)


def down_kernel(mine_ref, other_ref, keep_ref, recv_ref, o0, o1, o2, o3):
    rows = jnp.concatenate([mine_ref[...], other_ref[...]], axis=1)
    weights = jnp.concatenate([keep_ref[...], recv_ref[...]], axis=0)
    total = jnp.dot(rows, weights, preferred_element_type=F32)
    for step, out in enumerate((o0, o1, o2, o3)):
        out[...] = total[step * 128 : (step + 1) * 128].astype(out.dtype)


def make_down(mine, other, keep, recv):
    rows, width = mine.shape
    columns = keep.shape[1]
    step = 1024
    whole = lambda x: pl.BlockSpec(x.shape, lambda i: (0, 0))
    tile = lambda n: pl.BlockSpec((n, step), lambda i: (0, i))
    return pl.pallas_call(
        down_kernel,
        out_shape=[jax.ShapeDtypeStruct((rows // 4, columns), F32 if d == 0 else BF) for d in range(4)],
        grid=(columns // step,),
        in_specs=[whole(mine), whole(other), tile(width), tile(width)],
        out_specs=[tile(rows // 4)] * 4,
        compiler_params=pltpu.CompilerParams(vmem_limit_bytes=48 * 1024 * 1024),
        cost_estimate=pl.CostEstimate(
            flops=4 * rows * width * columns, bytes_accessed=9 * 1024 * 1024, transcendentals=0
        ),
    )(mine, other, keep, recv)


def local(
    query,
    fresh_token_keys,
    fresh_token_values,
    stored_keys,
    stored_values,
    slot_cache_length,
    residual,
    prenorm_scale,
    request_cache_slot,
    request_adapter,
    gate_projection_levels,
    gate_group_scales,
    up_projection_levels,
    up_group_scales,
    down_projection_levels,
    down_group_scales,
    adapter_input_maps,
    adapter_gate_maps,
):
    role = lax.axis_index("role")
    shard = lax.axis_index("shard")
    here = (shard // 16, (shard // 4) % 4, shard % 4)
    half = residual.shape[1]
    units = gate_projection_levels.shape[1]
    first = role == 0

    def axis_of(mine, phase):
        a, b = AXES[0][phase], AXES[1][phase]
        return (a, b) if mine else (b, a)

    def by_role(pair, values):
        return jnp.where(first, values[pair[0]], values[pair[1]])

    def position(slot, mine):
        q = slot // 8
        chip = (q // 16, (q // 4) % 4, q % 4)
        last, across = axis_of(mine, 2), axis_of(mine, 1)
        total = (by_role(last, here) - by_role(last, chip)) % 4
        return (total * 16 + chip[2] * 4 + by_role(across, chip)) * 8 + slot % 8

    every = jnp.arange(512, dtype=jnp.int32)
    pos_of_request = position(request_cache_slot, True)
    hit_row = pos_of_request[None, :] == every[:, None]
    adapter_of_row = jnp.sum(jnp.where(hit_row, request_adapter[None, :], 0), axis=1)
    def request_slots(mine):
        z, w = (every // 32) % 4, (every // 8) % 4
        far = (by_role(axis_of(mine, 2), here) + every // 128) % 4
        swapped = first if mine else jnp.logical_not(first)
        chip = chip_index((jnp.where(swapped, far, w), jnp.where(swapped, w, far), z))
        lane = every % 8
        return pick(request_cache_slot, (lane // 4) * 256 + chip * 4 + lane % 4)

    slots = request_slots(True)
    pos_mine = jnp.broadcast_to(position(slots, True)[:, None], (512, 128))
    pos_other = jnp.broadcast_to(position(request_slots(False), True)[:, None], (512, 128))
    own_place = here[2] * 4 + by_role(axis_of(True, 1), here)
    own_pos = position(lax.dynamic_slice(slots, (own_place * 8,), (8,)), True)
    own_pick = (own_pos[:, None] == every[None, :]).astype(BF)

    gain = prenorm_scale.astype(F32)
    maps_raw = adapter_input_maps.reshape(-1, 2 * half)
    maps_keep = lax.dynamic_slice(maps_raw, (0, role * half), (maps_raw.shape[0], half))
    maps_send = lax.dynamic_slice(maps_raw, (0, (1 - role) * half), (maps_raw.shape[0], half))
    maps_near = jnp.concatenate([maps_keep, swap(maps_send)], axis=0)
    last = axis_of(True, 2)

    def adapters_at(step, of_role):
        mine = [jnp.where(first, last[0], last[1]) == axis for axis in range(3)]
        chip = chip_index([jnp.where(m, (c + step) % 4, c) for m, c in zip(mine, here)])
        return (of_role * 64 + chip) * 2 + jnp.arange(2, dtype=jnp.int32)

    ids = jnp.concatenate([adapters_at(step, of) for step in (0, 2) for of in (role, 1 - role)])

    attended = attend(
        query,
        fresh_token_keys,
        fresh_token_values,
        stored_keys,
        stored_values,
        slot_cache_length,
        stored_keys.shape[2] // HD,
        HD,
    )
    stream = (residual.astype(F32) + attended).astype(BF)

    weights, down_keep, down_send, token = make_weights(
        role,
        gate_projection_levels,
        gate_group_scales,
        up_projection_levels,
        up_group_scales,
        gain.reshape(1, -1),
        down_projection_levels,
        down_group_scales,
        stream[:, :128],
    )
    maps_far = send(after(maps_near, stream), 2, 2)

    plane = exchange(jnp.broadcast_to(stream[None], (16,) + stream.shape)).reshape(128, half)
    plane = after(plane, token, maps_far)
    down_recv = swap(down_send)

    up = send(plane, 2, 1)
    down = send(plane, 2, -1)
    far_block = send(up, 2, 1)
    blocks = (plane, up, far_block, down)
    gain_half = lax.dynamic_slice(gain, (role * half,), (half,)).reshape(1, half)
    low_rows = jnp.concatenate([adapter_of_row[:256], adapter_of_row[384:]]).reshape(1, 384)
    low = make_low(ids, (plane, up, down), maps_near, maps_far, gain_half, low_rows)
    others = [swap(block) for block in (plane, up, down)]
    pick_first = jnp.concatenate([own_pick[:, :256], own_pick[:, 384:]], axis=1)
    *early, base = make_products((plane, up, down), others, weights, after(pick_first, low[0]))
    low = jnp.sum(after(exchange(low), early[0][None]), axis=0)
    far_other = swap(after(far_block, low))
    *late, base_far = make_products((far_block,), (far_other,), weights, own_pick[:, 256:384])
    got = ring(low, 2)
    column = {0: 0, 1: 128, 3: 256}
    sums = []
    for d in range(4):
        terms = [got[step][:, column[(d - step) % 4] :][:, :128] for step in range(4) if (d - step) % 4 != 2]
        sums.append(sum(terms[1:], terms[0]))
    low = jnp.concatenate(sums, axis=1)
    low_other = swap(low)

    ids_wide = jnp.broadcast_to(adapter_of_row[:, None], (512, 128))
    place = jnp.stack([by_role(axis_of(True, 2), here), by_role(axis_of(False, 2), here)])
    hidden, hidden_send = make_hidden(
        place, early, late, low, low_other, ids_wide, pos_mine, pos_other, adapter_gate_maps.reshape(-1, units)
    )
    hidden_other = swap(hidden_send)

    pieces = make_down(hidden, hidden_other, down_keep, down_recv)
    got = [send(pieces[step], 2, step) for step in (2, 1, 3)]
    total = pieces[0] + got[0].astype(F32) + got[1].astype(F32) + got[2].astype(F32)
    part = total.astype(BF).reshape(16, 8, half)
    total = jnp.sum(exchange(part).astype(F32), axis=0)
    result = (base + base_far + total).astype(BF)
    keep = lax.dynamic_slice(result, (role * 4, 0), (4, half))
    got = swap(lax.dynamic_slice(result, ((1 - role) * 4, 0), (4, half)))
    return jnp.concatenate([jnp.where(first, keep, got), jnp.where(first, got, keep)], axis=1)


def solution(mesh):
    return jax.shard_map(
        local,
        mesh=mesh,
        in_specs=(
            P("shard", "role"),
            P("shard", "role"),
            P("shard", "role"),
            P("shard", None, "role"),
            P("shard", None, "role"),
            P("shard"),
            P("shard", "role"),
            P(),
            P(),
            P(),
            P(None, ("role", "shard")),
            P(None, ("role", "shard")),
            P(None, ("role", "shard")),
            P(None, ("role", "shard")),
            P(("role", "shard"), None),
            P(("role", "shard"), None),
            P(("role", "shard"), None, None),
            P(None, None, ("role", "shard")),
        ),
        out_specs=P(("role", "shard"), None),
        check_vma=False,
    )
```

```python
import functools

import jax
import jax.numpy as jnp
from jax import lax
from jax.experimental import pallas as pl
from jax.experimental.pallas import tpu as pltpu
from jax.sharding import PartitionSpec as P

HD = 128
BF = jnp.bfloat16
F32 = jnp.float32
AXES = ((2, 1, 0), (2, 0, 1))


def attend(
    query,
    fresh_token_keys,
    fresh_token_values,
    stored_keys,
    stored_values,
    slot_cache_length,
    kv_heads,
    head_dim,
):
    rows = query.shape[0]
    length = stored_keys.shape[1]
    groups = query.shape[1] // (kv_heads * head_dim)
    queries = query.reshape(rows, kv_heads, groups, head_dim)
    keys = stored_keys.reshape(rows, length, kv_heads, head_dim)
    values = stored_values.reshape(rows, length, kv_heads, head_dim)
    own_keys = fresh_token_keys.reshape(rows, kv_heads, head_dim)
    own_values = fresh_token_values.reshape(rows, kv_heads, head_dim)
    factor = head_dim ** (-0.5)
    scores = jnp.einsum("skgd,slkd->skgl", queries, keys, preferred_element_type=F32) * factor
    valid = jnp.arange(length)[None, :] < slot_cache_length[:, None]
    scores = jnp.where(valid[:, None, None, :], scores, -1e30)
    own = jnp.einsum("skgd,skd->skg", queries, own_keys, preferred_element_type=F32) * factor
    top = jnp.maximum(jnp.max(scores, axis=-1), own)
    weights = jnp.exp(scores - top[..., None])
    own_weight = jnp.exp(own - top)
    total = jnp.sum(weights, axis=-1) + own_weight
    mixed = jnp.einsum("skgl,slkd->skgd", weights.astype(BF), values, preferred_element_type=F32)
    mixed = (
        mixed
        + own_weight.astype(BF).astype(F32)[..., None] * own_values.astype(F32)[:, :, None, :]
    )
    return (mixed / total[..., None]).reshape(rows, -1)


def dequant(levels, scales):
    count, cols = levels.shape
    blocks = scales.shape[0]
    wide = levels.reshape(blocks, count // blocks, cols).astype(F32) * scales[:, None, :]
    return wide.reshape(count, cols).astype(BF)


def weights_kernel(role, gate_ref, gate_scale, up_ref, up_scale, gain_ref, down_ref, down_scale, ready, out_ref, keep_ref, send_ref, token):
    width = gate_ref.shape[1]
    for group in range(gate_ref.shape[0] // 128):
        rows = slice(group * 128, (group + 1) * 128)
        gain = jnp.broadcast_to(gain_ref[0:1, rows], (128, 128)).T
        gain = jnp.concatenate([gain] * (width // 128), axis=1)
        for place, (levels, scales) in enumerate(((gate_ref, gate_scale), (up_ref, up_scale))):
            wide = (levels[rows, :].astype(F32) * scales[group : group + 1, :]).astype(BF)
            out_ref[rows, place * width : (place + 1) * width] = (wide.astype(F32) * gain).astype(BF)
    i = pl.program_id(0)
    half = pl.num_programs(0) // 2
    for ref, here in ((keep_ref, i < half), (send_ref, i >= half)):

        @pl.when(here)
        def _():
            for group in range(down_ref.shape[0] // 128):
                rows = slice(group * 128, (group + 1) * 128)
                ref[rows, :] = (down_ref[rows, :].astype(F32) * down_scale[group : group + 1, :]).astype(BF)

    token[...] = jnp.zeros_like(token)


def make_weights(role, gate, gate_scales, up, up_scales, gain, down, down_scales, ready):
    depth, width = gate.shape
    step = 1024
    count = depth // step
    half = count // 2
    turned = lambda i, r: (i + r[0] * half) % count
    levels = pl.BlockSpec((step, width), lambda i, r: (turned(i, r), 0))
    scales = pl.BlockSpec((step // 128, width), lambda i, r: (turned(i, r), 0))
    across = lambda rows: pl.BlockSpec((rows, step), lambda i, r: (0, turned(i, r)))
    return pl.pallas_call(
        weights_kernel,
        out_shape=[
            jax.ShapeDtypeStruct((depth, 2 * width), BF),
            jax.ShapeDtypeStruct((width, depth // 2), BF),
            jax.ShapeDtypeStruct((width, depth // 2), BF),
            jax.ShapeDtypeStruct((16, 128), BF),
        ],
        grid_spec=pltpu.PrefetchScalarGridSpec(
            num_scalar_prefetch=1,
            grid=(count,),
            in_specs=[levels, scales, levels, scales, across(1), across(width), across(down_scales.shape[0]), pl.BlockSpec((8, 128), lambda i, r: (0, 0))],
            out_specs=[
                pl.BlockSpec((step, 2 * width), lambda i, r: (i, 0)),
                pl.BlockSpec((width, step), lambda i, r: (0, jnp.minimum(i, half - 1))),
                pl.BlockSpec((width, step), lambda i, r: (0, jnp.maximum(i - half, 0))),
                pl.BlockSpec((16, 128), lambda i, r: (0, 0)),
            ],
        ),
        compiler_params=pltpu.CompilerParams(vmem_limit_bytes=48 * 1024 * 1024),
        cost_estimate=pl.CostEstimate(flops=12 * depth * width, bytes_accessed=12 * depth * width, transcendentals=0),
    )(role.reshape(1), gate, gate_scales, up, up_scales, gain, down, down_scales, ready)


def chip_index(coords):
    return coords[0] * 16 + coords[1] * 4 + coords[2]


def shift_perm(phase, step):
    pairs = []
    for role in range(2):
        axis = AXES[role][phase]
        for x in range(4):
            for y in range(4):
                for z in range(4):
                    here = [x, y, z]
                    there = list(here)
                    there[axis] = (there[axis] + step) % 4
                    pairs.append((role * 64 + chip_index(here), role * 64 + chip_index(there)))
    return pairs


def send(value, phase, step):
    return lax.ppermute(value, ("role", "shard"), shift_perm(phase, step))


def swap(value):
    return lax.ppermute(value, "role", [(0, 1), (1, 0)])


def plane_groups():
    groups = []
    for role in range(2):
        across, last = AXES[role][1], AXES[role][2]
        for fixed in range(4):
            group = []
            for z in range(4):
                for w in range(4):
                    coords = [0, 0, z]
                    coords[across], coords[last] = w, fixed
                    group.append(role * 64 + chip_index(coords))
            groups.append(group)
    return groups


def exchange(value):
    return lax.all_to_all(value, ("role", "shard"), 0, 0, axis_index_groups=plane_groups())


def ring(value, phase):
    return [value] + [send(value, phase, step) for step in (1, 2, 3)]


def after(value, *others):
    for other in others:
        cut = other[tuple(slice(0, min(n, m)) for n, m in zip(value.shape, other.shape))]
        zero = (cut * 0).astype(value.dtype)
        value = value + jnp.pad(zero, [(0, n - m) for n, m in zip(value.shape, zero.shape)])
    return value


def pick(table, index):
    hit = index[:, None] == jnp.arange(table.shape[0], dtype=jnp.int32)[None, :]
    return jnp.sum(jnp.where(hit, table[None, :], 0), axis=1)


def low_kernel(ids, x0, x1, x3, near_ref, far_ref, gain_ref, rows_ref, out_ref):
    gain = gain_ref[...].astype(F32)
    near = (near_ref[...].astype(F32) * gain).astype(BF)
    far = (far_ref[...].astype(F32) * gain).astype(BF)
    turn = (((1,), (1,)), ((), ()))
    parts = []
    for place, x in enumerate((x0, x1, x3)):
        block = x[...]
        rows = rows_ref[0:1, place * 128 : (place + 1) * 128]
        total = jnp.zeros((16, 128), F32)
        for base, table in ((0, near), (4, far)):
            if base == 4 and place > 0:
                continue
            got = lax.dot_general(table, block, turn, preferred_element_type=F32)
            for entry in range(4):
                total = total + jnp.where(rows == ids[base + entry], got[entry * 16 : (entry + 1) * 16, :], 0.0)
        parts.append(total)
    low = jnp.concatenate(parts, axis=1)
    for copy in range(16):
        out_ref[copy] = low


def make_low(ids, blocks, near, far, gain, rows):
    whole = pl.BlockSpec(memory_space=pltpu.VMEM)
    return pl.pallas_call(
        low_kernel,
        out_shape=jax.ShapeDtypeStruct((16, 16, 384), F32),
        in_specs=[pl.BlockSpec(memory_space=pltpu.SMEM)] + [whole] * 7,
        out_specs=whole,
        compiler_params=pltpu.CompilerParams(vmem_limit_bytes=48 * 1024 * 1024),
        cost_estimate=pl.CostEstimate(flops=2 * 256 * 128 * 4096, bytes_accessed=5 * 1024 * 1024, transcendentals=0),
    )(ids, *blocks, near, far, gain, rows)


def products_kernel(count, *refs):
    mine, others = refs[:count], refs[count : 2 * count]
    w_mine, w_other, pick_ref, own, other, own_sq, other_sq, base = refs[2 * count :]

    @pl.when(pl.program_id(0) == 0)
    def _():
        own[...] = jnp.zeros_like(own)
        other[...] = jnp.zeros_like(other)
        own_sq[...] = jnp.zeros_like(own_sq)
        other_sq[...] = jnp.zeros_like(other_sq)

    for parts, weights, out, square in ((mine, w_mine, own, own_sq), (others, w_other, other, other_sq)):
        x = jnp.concatenate([part[...] for part in parts], axis=0)
        out[...] += jnp.dot(x, weights[...], preferred_element_type=F32)
        wide = x.astype(F32)
        wide = wide * wide
        square[...] += sum(wide[:, i * 128 : (i + 1) * 128] for i in range(wide.shape[1] // 128))
        if out is own:
            base[...] = jnp.dot(pick_ref[...], x, preferred_element_type=F32)


def make_products(mine, others, weights, pick):
    step = 1024
    depth, width = weights.shape[0] // 2, weights.shape[1]
    count = len(mine)
    rows = 128 * count
    x_spec = pl.BlockSpec((128, step), lambda k: (0, k))
    mine_spec = pl.BlockSpec((step, width), lambda k: (k, 0))
    other_spec = pl.BlockSpec((step, width), lambda k: (k + depth // step, 0))
    fixed = lambda *shape: pl.BlockSpec(shape, lambda k: (0, 0))
    return pl.pallas_call(
        functools.partial(products_kernel, count),
        out_shape=[
            jax.ShapeDtypeStruct((rows, width), F32),
            jax.ShapeDtypeStruct((rows, width), F32),
            jax.ShapeDtypeStruct((rows, 128), F32),
            jax.ShapeDtypeStruct((rows, 128), F32),
            jax.ShapeDtypeStruct((8, depth), F32),
        ],
        grid=(depth // step,),
        in_specs=[x_spec] * (2 * count) + [mine_spec, other_spec, fixed(8, rows)],
        out_specs=[fixed(rows, width), fixed(rows, width), fixed(rows, 128), fixed(rows, 128), pl.BlockSpec((8, step), lambda k: (0, k))],
        compiler_params=pltpu.CompilerParams(vmem_limit_bytes=48 * 1024 * 1024),
        cost_estimate=pl.CostEstimate(
            flops=4 * rows * depth * width, bytes_accessed=(12 + 2 * count) * 1024 * 1024, transcendentals=0
        ),
    )(*mine, *others, weights, weights, pick)


def hidden_kernel(place, own_a, other_a, own_sq_a, other_sq_a, own_b, other_b, own_sq_b, other_sq_b, low_ref, low_other, ids_ref, pos_mine, pos_other, maps_ref, out_ref, out_other, low_got, sq, hidden, other, other_sq):
    def there(d, z, w):
        row = ((place[1] - w) & 3) * 128 + z * 32 + ((place[0] - d) & 3) * 8
        return pl.ds(pl.multiple_of(row, 8), 8)

    for part_a, part_b, into in ((other_a, other_b, other), (other_sq_a, other_sq_b, other_sq)):
        into[0:256, :] = part_a[0:256, :]
        into[256:384, :] = part_b[...]
        into[384:512, :] = part_a[256:384, :]
    source = lambda d: (d == 2, (0, 128, 0, 256)[d])
    fill = jnp.zeros((112, 512), F32)
    low_got[...] = jnp.concatenate([low_other[...], fill], axis=0).T
    low_mine = jnp.concatenate([low_ref[...], fill], axis=0).T
    parts = []
    for d in range(4):
        for z in range(4):
            for w in range(4):
                row = d * 128 + z * 32 + w * 8
                second, start = source(d)
                mine = (own_sq_b if second else own_sq_a)[start + z * 32 + w * 8 : start + z * 32 + w * 8 + 8, :]
                sq[row : row + 8, :] = mine + other_sq[there(d, z, w), :]
                parts.append(low_got[there(d, z, w), :])
    inv = lax.rsqrt(jnp.sum(sq[...], axis=1, keepdims=True) / 8192.0 + 1e-05)
    total = low_mine + jnp.concatenate(parts, axis=0)
    column = lax.broadcasted_iota(jnp.int32, (128, 128), 0)
    lane = lax.broadcasted_iota(jnp.int32, (128, 128), 1)
    spread = jnp.where(column == lane % 16, 1.0, 0.0).astype(BF)
    low = jnp.dot((total * inv).astype(BF), spread, preferred_element_type=F32)
    inv = jnp.broadcast_to(inv, (512, 128))
    lane = lax.broadcasted_iota(jnp.int32, (512, 128), 1)
    rest = ids_ref[...] - lane // 16
    acc = jnp.zeros(out_ref.shape, F32)
    for j in range(16):
        sides = [jnp.where(rest == 8 * (2 * j + i), low, 0.0).astype(BF) for i in range(2)]
        lhs = jnp.concatenate(sides, axis=1)
        acc = acc + jnp.dot(lhs, maps_ref[j * 256 : (j + 1) * 256, :], preferred_element_type=F32)
    width = out_ref.shape[1]
    for d in range(4):
        for z in range(4):
            for v in range(2):
                row = d * 128 + z * 32 + v * 16
                sums = [other[there(d, z, w), :] for w in (2 * v, 2 * v + 1)]
                second, start = source(d)
                start = start + z * 32 + v * 16
                both = (own_b if second else own_a)[start : start + 16, :] + jnp.concatenate(sums, axis=0)
                scale = jnp.concatenate([inv[row : row + 16, :]] * (width // 128), axis=1)
                gate = both[:, :width] * scale + 2.0 * acc[row : row + 16, :]
                up = both[:, width:] * scale
                hidden[row : row + 16, :] = (gate / (1.0 + jnp.exp(-gate)) * up).astype(BF)
    value = hidden[...]
    for pos_ref, out in ((pos_mine, out_ref), (pos_other, out_other)):
        pos = pos_ref[...]
        pick = jnp.concatenate([jnp.where(pos == lane + 128 * i, 1.0, 0.0).astype(BF) for i in range(4)], axis=1)
        out[...] = jnp.dot(pick, value, preferred_element_type=F32).astype(BF)


def make_hidden(place, first, second, low, low_other, ids, pos_mine, pos_other, maps):
    rows = 512
    width = maps.shape[1]
    whole = pl.BlockSpec(memory_space=pltpu.VMEM)
    return pl.pallas_call(
        hidden_kernel,
        out_shape=[jax.ShapeDtypeStruct((rows, width), BF)] * 2,
        in_specs=[pl.BlockSpec(memory_space=pltpu.SMEM)] + [whole] * 14,
        out_specs=[whole] * 2,
        scratch_shapes=[pltpu.VMEM((rows, 128), F32), pltpu.VMEM((rows, 128), F32), pltpu.VMEM((rows, width), BF), pltpu.VMEM((rows, 2 * width), F32), pltpu.VMEM((rows, 128), F32)],
        compiler_params=pltpu.CompilerParams(vmem_limit_bytes=48 * 1024 * 1024),
        cost_estimate=pl.CostEstimate(
            flops=2 * rows * 4096 * width, bytes_accessed=6 * 1024 * 1024, transcendentals=rows * width
        ),
    )(place, *first, *second, low, low_other, ids, pos_mine, pos_other, maps)


def down_kernel(mine_ref, other_ref, keep_ref, recv_ref, *outs):
    rows = jnp.concatenate([mine_ref[...], other_ref[...]], axis=1)
    weights = jnp.concatenate([keep_ref[...], recv_ref[...]], axis=0)
    total = jnp.dot(rows, weights, preferred_element_type=F32)
    i = pl.program_id(0)
    half = pl.num_programs(0) // 2
    for group, here in ((outs[:4], i < half), (outs[4:], i >= half)):

        @pl.when(here)
        def _():
            for step, out in enumerate(group):
                out[...] = total[step * 128 : (step + 1) * 128].astype(out.dtype)


def make_down(mine, other, keep, recv):
    rows, width = mine.shape
    columns = keep.shape[1]
    step = 1024
    half = columns // step // 2
    whole = lambda x: pl.BlockSpec(x.shape, lambda i: (0, 0))
    tile = pl.BlockSpec((width, step), lambda i: (0, i))
    left = pl.BlockSpec((rows // 4, step), lambda i: (0, jnp.minimum(i, half - 1)))
    right = pl.BlockSpec((rows // 4, step), lambda i: (0, jnp.maximum(i - half, 0)))
    kinds = [F32, BF, BF, BF] * 2
    return pl.pallas_call(
        down_kernel,
        out_shape=[jax.ShapeDtypeStruct((rows // 4, columns // 2), kind) for kind in kinds],
        grid=(columns // step,),
        in_specs=[whole(mine), whole(other), tile, tile],
        out_specs=[left] * 4 + [right] * 4,
        compiler_params=pltpu.CompilerParams(vmem_limit_bytes=48 * 1024 * 1024),
        cost_estimate=pl.CostEstimate(
            flops=4 * rows * width * columns, bytes_accessed=9 * 1024 * 1024, transcendentals=0
        ),
    )(mine, other, keep, recv)


def local(
    query,
    fresh_token_keys,
    fresh_token_values,
    stored_keys,
    stored_values,
    slot_cache_length,
    residual,
    prenorm_scale,
    request_cache_slot,
    request_adapter,
    gate_projection_levels,
    gate_group_scales,
    up_projection_levels,
    up_group_scales,
    down_projection_levels,
    down_group_scales,
    adapter_input_maps,
    adapter_gate_maps,
):
    role = lax.axis_index("role")
    shard = lax.axis_index("shard")
    here = (shard // 16, (shard // 4) % 4, shard % 4)
    half = residual.shape[1]
    units = gate_projection_levels.shape[1]
    first = role == 0

    def axis_of(mine, phase):
        a, b = AXES[0][phase], AXES[1][phase]
        return (a, b) if mine else (b, a)

    def by_role(pair, values):
        return jnp.where(first, values[pair[0]], values[pair[1]])

    def position(slot, mine):
        q = slot // 8
        chip = (q // 16, (q // 4) % 4, q % 4)
        last, across = axis_of(mine, 2), axis_of(mine, 1)
        total = (by_role(last, here) - by_role(last, chip)) % 4
        return (total * 16 + chip[2] * 4 + by_role(across, chip)) * 8 + slot % 8

    every = jnp.arange(512, dtype=jnp.int32)
    pos_of_request = position(request_cache_slot, True)
    hit_row = pos_of_request[None, :] == every[:, None]
    adapter_of_row = jnp.sum(jnp.where(hit_row, request_adapter[None, :], 0), axis=1)
    def request_slots(mine):
        z, w = (every // 32) % 4, (every // 8) % 4
        far = (by_role(axis_of(mine, 2), here) + every // 128) % 4
        swapped = first if mine else jnp.logical_not(first)
        chip = chip_index((jnp.where(swapped, far, w), jnp.where(swapped, w, far), z))
        lane = every % 8
        return pick(request_cache_slot, (lane // 4) * 256 + chip * 4 + lane % 4)

    slots = request_slots(True)
    pos_mine = jnp.broadcast_to(position(slots, True)[:, None], (512, 128))
    pos_other = jnp.broadcast_to(position(request_slots(False), True)[:, None], (512, 128))
    own_place = here[2] * 4 + by_role(axis_of(True, 1), here)
    own_pos = position(lax.dynamic_slice(slots, (own_place * 8,), (8,)), True)
    own_pick = (own_pos[:, None] == every[None, :]).astype(BF)

    gain = prenorm_scale.astype(F32)
    maps_raw = adapter_input_maps.reshape(-1, 2 * half)
    maps_keep = lax.dynamic_slice(maps_raw, (0, role * half), (maps_raw.shape[0], half))
    maps_send = lax.dynamic_slice(maps_raw, (0, (1 - role) * half), (maps_raw.shape[0], half))
    maps_near = jnp.concatenate([maps_keep, swap(maps_send)], axis=0)
    last = axis_of(True, 2)

    def adapters_at(step, of_role):
        mine = [jnp.where(first, last[0], last[1]) == axis for axis in range(3)]
        chip = chip_index([jnp.where(m, (c + step) % 4, c) for m, c in zip(mine, here)])
        return (of_role * 64 + chip) * 2 + jnp.arange(2, dtype=jnp.int32)

    ids = jnp.concatenate([adapters_at(step, of) for step in (0, 2) for of in (role, 1 - role)])

    attended = attend(
        query,
        fresh_token_keys,
        fresh_token_values,
        stored_keys,
        stored_values,
        slot_cache_length,
        stored_keys.shape[2] // HD,
        HD,
    )
    stream = (residual.astype(F32) + attended).astype(BF)

    weights, down_keep, down_send, token = make_weights(
        role,
        gate_projection_levels,
        gate_group_scales,
        up_projection_levels,
        up_group_scales,
        gain.reshape(1, -1),
        down_projection_levels,
        down_group_scales,
        stream[:, :128],
    )
    maps_far = send(after(maps_near, stream), 2, 2)

    plane = exchange(jnp.broadcast_to(stream[None], (16,) + stream.shape)).reshape(128, half)
    plane = after(plane, token, maps_far)
    down_recv = swap(down_send)

    up = send(plane, 2, 1)
    down = send(plane, 2, -1)
    far_block = send(up, 2, 1)
    blocks = (plane, up, far_block, down)
    gain_half = lax.dynamic_slice(gain, (role * half,), (half,)).reshape(1, half)
    low_rows = jnp.concatenate([adapter_of_row[:256], adapter_of_row[384:]]).reshape(1, 384)
    low = make_low(ids, (plane, up, down), maps_near, maps_far, gain_half, low_rows)
    others = [swap(block) for block in (plane, up, down)]
    pick_first = jnp.concatenate([own_pick[:, :256], own_pick[:, 384:]], axis=1)
    *early, base = make_products((plane, up, down), others, weights, after(pick_first, low[0]))
    low = jnp.sum(after(exchange(low), early[0][None]), axis=0)
    far_other = swap(after(far_block, low))
    *late, base_far = make_products((far_block,), (far_other,), weights, own_pick[:, 256:384])
    got = ring(low, 2)
    column = {0: 0, 1: 128, 3: 256}
    sums = []
    for d in range(4):
        terms = [got[step][:, column[(d - step) % 4] :][:, :128] for step in range(4) if (d - step) % 4 != 2]
        sums.append(sum(terms[1:], terms[0]))
    low = jnp.concatenate(sums, axis=1)
    low_other = swap(low)

    ids_wide = jnp.broadcast_to(adapter_of_row[:, None], (512, 128))
    place = jnp.stack([by_role(axis_of(True, 2), here), by_role(axis_of(False, 2), here)])
    hidden, hidden_send = make_hidden(
        place, early, late, low, low_other, ids_wide, pos_mine, pos_other, adapter_gate_maps.reshape(-1, units)
    )
    hidden_other = swap(hidden_send)

    pieces = make_down(hidden, hidden_other, down_keep, down_recv)
    totals = []
    for side in (pieces[:4], pieces[4:]):
        got = [send(side[step], 2, step) for step in (2, 1, 3)]
        total = side[0] + got[0].astype(F32) + got[1].astype(F32) + got[2].astype(F32)
        total = exchange(total.astype(BF).reshape(16, 8, half // 2))
        totals.append(jnp.sum(total.astype(F32), axis=0))
    total = jnp.concatenate(totals, axis=1)
    result = (base + base_far + total).astype(BF)
    keep = lax.dynamic_slice(result, (role * 4, 0), (4, half))
    got = swap(lax.dynamic_slice(result, ((1 - role) * 4, 0), (4, half)))
    return jnp.concatenate([jnp.where(first, keep, got), jnp.where(first, got, keep)], axis=1)


def solution(mesh):
    return jax.shard_map(
        local,
        mesh=mesh,
        in_specs=(
            P("shard", "role"),
            P("shard", "role"),
            P("shard", "role"),
            P("shard", None, "role"),
            P("shard", None, "role"),
            P("shard"),
            P("shard", "role"),
            P(),
            P(),
            P(),
            P(None, ("role", "shard")),
            P(None, ("role", "shard")),
            P(None, ("role", "shard")),
            P(None, ("role", "shard")),
            P(("role", "shard"), None),
            P(("role", "shard"), None),
            P(("role", "shard"), None, None),
            P(None, None, ("role", "shard")),
        ),
        out_specs=P(("role", "shard"), None),
        check_vma=False,
    )
```
